256 devices in a mesh: group: 4 (over z_lo, core), tile: 64 (over x, z_hi, y).
Axes of the slice: x: 4, y: 4, z: 8 (z_hi: 4, z_lo: 2; z = z_hi * 2 + z_lo), core: 2. Of those that a mesh axis runs over, the one named last changes fastest.
Arguments:
- object_slices: bfloat16 [4, 2048, 8192], P(None, 'group', 'tile'), may hold values from -4 to 4
- probe: float32 [1024, 256], replicated, may hold values from -6 to 6
- mid_waves: bfloat16 [4, 64, 3, 2, 2, 256, 256], P('group', 'tile'), may hold values from -160 to 160
- amplitudes: bfloat16 [4, 64, 3, 256, 256], P('group', 'tile'), may hold values from 0.19921875 to 4
- row_offsets: int32 [4, 64, 3], P('group', 'tile'), may hold values from 0 to 256
- col_offsets: int32 [4, 64, 3], P('group', 'tile'), may hold values from 0 to 128
Outputs:
- object_new: float32 [4, 2048, 8192], P(None, 'group', 'tile')
- probe_new: float32 [1024, 256], P('tile')
The draws below stay inside these ranges and needn't reach their ends.
All inputs are finite; a program needn't handle non-finite values.
Results may differ from the reference program's by a relative error of at most 0.0003.
Values may be sent and summed in bfloat16 or wider, within the bound.
A program may use at most 128 MiB of HBM per device.

```python
import math
import jax
import jax.numpy as jnp
from jax import lax

PX = 256
MODES = 2
POS_DEV = 3
ROWS = 512
COLS_DEV = 128
GROUPS = 4
TILES = 64
NR = 2048
NC = 8192


def draw_mid_waves(key, part):
    shape = (GROUPS, TILES, POS_DEV, 2, MODES, PX, PX)
    total = GROUPS * TILES
    ranking = (jnp.arange(total, dtype=jnp.float32) / max(total - 1, 1)).reshape(GROUPS, TILES, 1, 1, 1, 1, 1)
    values = jnp.clip(jax.random.normal(key, shape, jnp.float32), -5.0, 5.0)
    return (values * (1.0 + 2.0 * ranking)).astype(jnp.bfloat16)


def set_ends(array, key, smallest, high):
    spot = [jax.random.randint(jax.random.fold_in(key, axis), (), 0, length) for axis, length in enumerate(array.shape)]
    widest = array.shape.index(max(array.shape))
    beside = spot[:widest] + [(spot[widest] + 1) % array.shape[widest]] + spot[widest + 1:]
    return array.at[tuple(spot)].set(smallest).at[tuple(beside)].set(high)


def level_of(own_key, dims, shards, smallest, largest):
    loudness = 1.0
    for dim, shards_of in shards:
        draws = jax.random.uniform(jax.random.fold_in(jax.random.fold_in(own_key, 6), dim), (shards_of,), jnp.float32, smallest / len(shards), largest / len(shards))
        loudness = loudness * jnp.repeat(jnp.exp(draws), dims[dim] // shards_of).reshape((-1,) + (1,) * (len(dims) - 1 - dim))
    return loudness


def bell_draw(stream_key, dims, width, bound, pieces=(), kind=jnp.bfloat16):
    drawn = width * jax.random.normal(stream_key, dims, jnp.float32)
    if pieces:
        drawn = drawn * level_of(stream_key, dims, pieces, -0.22, 0.18)
    return jnp.clip(drawn, -bound, bound).astype(kind)


def setup_inputs(seed: int = 0) -> dict:
    splits = jax.random.split(jax.random.key(seed), 7)
    return {
        "object_slices": bell_draw(splits[0], (4, NR, NC), 0.7, 4.0, ((1, 4), (2, 64))),
        "probe": bell_draw(splits[1], (2 * MODES * PX, PX), 1.0, 6.0, (), jnp.float32),
        "mid_waves": draw_mid_waves(jax.random.fold_in(splits[6], 71), 0),
        "amplitudes": jnp.clip(jnp.exp(math.log(4.0) - 2.9996462 * jax.random.uniform(splits[3], (GROUPS, TILES, POS_DEV, PX, PX), jnp.float32) ** level_of(splits[3], (GROUPS, TILES, POS_DEV, PX, PX), ((0, 4), (1, 64)), -0.2, 0.2)), 0.19921875, 4.0).astype(jnp.bfloat16),
        "row_offsets": set_ends(jax.random.randint(splits[4], (GROUPS, TILES, POS_DEV), 0, ROWS - PX + 1), jax.random.fold_in(splits[4], 1), 0, ROWS - PX).astype(jnp.int32),
        "col_offsets": set_ends(jax.random.randint(splits[5], (GROUPS, TILES, POS_DEV), 0, 3 * COLS_DEV - PX + 1), jax.random.fold_in(splits[5], 1), 0, 3 * COLS_DEV - PX).astype(jnp.int32),
    }


phase_rate = 0.25
floor_level = 0.5
object_step = 0.5
probe_step = 0.5
epsilon = 1e-06

def back_kernel():
    freq = jnp.arange(PX, dtype=jnp.int32)
    freq = jnp.where(freq < PX // 2, freq, freq - PX).astype(jnp.float32)
    phase = 2.0 * jnp.pi * phase_rate / PX * (freq[:, None] * freq[:, None] + freq[None, :] * freq[None, :])
    return jnp.cos(phase) + 1j * jnp.sin(phase)

def reference(object_slices, probe, mid_waves, amplitudes, row_offsets, col_offsets):
    obj = object_slices.astype(jnp.float32)
    padded = jnp.pad(obj, ((0, 0), (0, 0), (COLS_DEV, COLS_DEV)))
    probe_parts = probe.reshape(2, MODES, PX, PX)
    probe_cplx = probe_parts[0] + 1j * probe_parts[1]
    kernel = back_kernel()

    def visit(state_sum, device):
        grad_obj, grad_probe = state_sum
        grp = device // TILES
        til = device % TILES
        for position in range(POS_DEV):
            row_at = grp * ROWS + row_offsets[grp, til, position]
            col_at = til * COLS_DEV + col_offsets[grp, til, position]
            patch = lax.dynamic_slice(padded, (jnp.int32(0), row_at, col_at), (4, PX, PX))
            first = patch[0] + 1j * patch[1]
            second = patch[2] + 1j * patch[3]
            wave = mid_waves[grp, til, position].astype(jnp.float32)
            middle = wave[0] + 1j * wave[1]
            amp = amplitudes[grp, til, position].astype(jnp.float32)
            far = jnp.fft.fft2(middle * second[None], norm='ortho')
            power = lax.optimization_barrier(jnp.sum(jnp.real(far) ** 2 + jnp.imag(far) ** 2, axis=0))
            magnitude = jnp.maximum(jnp.sqrt(power), floor_level)
            chi = jnp.fft.ifft2(far * (1.0 - amp / magnitude)[None], norm='ortho')
            grad_second = lax.optimization_barrier(jnp.sum(jnp.conj(middle) * chi, axis=0))
            spectrum = jnp.fft.fft2(jnp.conj(second)[None] * chi, norm='ortho')
            back_wave = jnp.fft.ifft2(spectrum * kernel[None], norm='ortho')
            grad_first = lax.optimization_barrier(jnp.sum(jnp.conj(probe_cplx) * back_wave, axis=0))
            probe_term = jnp.conj(first)[None] * back_wave
            update = jnp.stack([jnp.real(grad_first), jnp.imag(grad_first), jnp.real(grad_second), jnp.imag(grad_second)])
            old = lax.dynamic_slice(grad_obj, (jnp.int32(0), row_at, col_at), (4, PX, PX))
            grad_obj = lax.dynamic_update_slice(grad_obj, old + update, (jnp.int32(0), row_at, col_at))
            grad_probe = grad_probe + jnp.stack([jnp.real(probe_term), jnp.imag(probe_term)])
        return ((grad_obj, grad_probe), None)
    start = (jnp.zeros(padded.shape, jnp.float32), jnp.zeros((2, MODES, PX, PX), jnp.float32))
    (grad_obj, grad_probe), _ = lax.scan(visit, start, jnp.arange(GROUPS * TILES, dtype=jnp.int32))
    grad_obj = grad_obj[:, :, COLS_DEV:COLS_DEV + NC]
    obj_rms = jnp.sqrt(jnp.sum(grad_obj * grad_obj) / (4 * NR * NC) + epsilon)
    object_new = obj - object_step * grad_obj / obj_rms
    grad_probe = grad_probe.reshape(2 * MODES * PX, PX)
    probe_rms = jnp.sqrt(jnp.sum(grad_probe * grad_probe) / (2 * MODES * PX * PX) + epsilon)
    probe_new = probe - probe_step * grad_probe / probe_rms
    return (object_new, probe_new)
```

```python
import numpy as np
import ml_dtypes
import jax
import jax.numpy as jnp
from jax import lax
from jax.sharding import PartitionSpec as P
from jax.experimental import pallas as pl
from jax.experimental.pallas import tpu as pltpu

phase_rate = 0.25
floor_level = 0.5
object_step = 0.5
probe_step = 0.5
epsilon = 1e-06
f32 = jnp.float32
bf16 = jnp.bfloat16
PX = 256
HALF = 128
TALL = PX + 8


def right_form(m):
    return np.block([[m.real, m.imag], [-m.imag, m.real]])


def left_form(m):
    return np.block([[m.real, -m.imag], [m.imag, m.real]])


def transform_tables():
    n = np.arange(HALF)[:, None]
    k = np.arange(HALF)[None, :]
    root = -2j * np.pi / PX
    even = np.exp(root * ((2 * n * k) % PX)) / np.sqrt(PX)
    odd = np.exp(root * ((n * (2 * k + 1)) % PX)) / np.sqrt(PX)
    freq = np.arange(PX)
    freq = np.where(freq < HALF, freq, freq - PX)
    phase = np.exp(2j * np.pi * phase_rate * freq * freq / PX)
    ring = np.fft.ifft(phase)
    i, j = np.meshgrid(np.arange(HALF), np.arange(HALF), indexing="ij")
    near, far = ring[(i - j) % PX], ring[(i - j + HALF) % PX]
    plus, minus = (near + far) / 2, (near - far) / 2
    forms = [
        right_form(even), right_form(odd),
        left_form(even.T), left_form(odd.T),
        left_form(even.conj()), left_form(odd.conj()),
        right_form(even.conj().T), right_form(odd.conj().T),
        right_form(plus.T), right_form(minus.T),
        left_form(plus), left_form(minus),
    ]
    whole = np.stack(forms)
    high = whole.astype(ml_dtypes.bfloat16)
    low = (whole - high.astype(np.float64)).astype(ml_dtypes.bfloat16)
    return np.stack([high, low], axis=1)


def split(x):
    high = x.astype(bf16)
    return high, (x - high.astype(f32)).astype(bf16)


def by_right(x, tables, index):
    high, low = split(x)
    t = tables[index, 0]
    return jnp.dot(
        jnp.concatenate([high, low, high], axis=1),
        jnp.concatenate([t, t, tables[index, 1]], axis=0),
        preferred_element_type=f32,
    )


def by_left(x, tables, index):
    high, low = split(x)
    t = tables[index, 0]
    return jnp.dot(
        jnp.concatenate([t, t, tables[index, 1]], axis=1),
        jnp.concatenate([high, low, high], axis=0),
        preferred_element_type=f32,
    )


def lanes(a, b):
    return jnp.concatenate([a, b], axis=1)


def rows(a, b):
    return jnp.concatenate([a, b], axis=0)


def halves(re, im):
    return lanes(re[:, :HALF], im[:, :HALF]), lanes(re[:, HALF:], im[:, HALF:])


def compute_kernel(row_ref, col_ref, mid_obj, left_obj, right_obj, probe, waves, amps, tables,
                   own, left_rim, right_rim, grad_probe,
                   obj, grad, patch, far, upd):
    obj[:, :512, :HALF] = left_obj[...].astype(f32)
    obj[:, :512, HALF : 2 * HALF] = mid_obj[...].astype(f32)
    obj[:, :512, 2 * HALF :] = right_obj[...].astype(f32)
    obj[:, 512:, :] = jnp.zeros((4, 8, 3 * HALF), f32)
    grad[...] = jnp.zeros_like(grad)
    grad_probe[...] = jnp.zeros_like(grad_probe)
    at_row = lax.broadcasted_iota(jnp.int32, (PX, PX), 0)
    at_col = lax.broadcasted_iota(jnp.int32, (PX, PX), 1)
    sort_row = (at_col == jnp.where(at_row < HALF, 2 * at_row, 2 * at_row - PX + 1)).astype(f32).astype(bf16)
    sort_col = (at_row == jnp.where(at_col < HALF, 2 * at_col, 2 * at_col - PX + 1)).astype(f32).astype(bf16)

    def visit(p, carry):
        row_at = row_ref[p]
        col_at = col_ref[p]
        row_base = pl.multiple_of(row_at // 8 * 8, 8)
        row_rest = row_at - row_base
        pick = (
            lax.broadcasted_iota(jnp.int32, (3 * HALF, PX), 0)
            == lax.broadcasted_iota(jnp.int32, (3 * HALF, PX), 1) + col_at
        ).astype(f32).astype(bf16)
        place = (
            lax.broadcasted_iota(jnp.int32, (PX, 3 * HALF), 1)
            == lax.broadcasted_iota(jnp.int32, (PX, 3 * HALF), 0) + col_at
        ).astype(f32).astype(bf16)
        for c in range(4):
            raw = obj[c, pl.ds(row_base, TALL), :].astype(bf16)
            wide = jnp.dot(raw, pick, preferred_element_type=f32)
            patch[c] = pltpu.roll(wide, TALL - row_rest, 0)[:PX]
        for m in range(2):
            sr, si = patch[2], patch[3]
            wr, wi = waves[p, 0, m].astype(f32), waves[p, 1, m].astype(f32)
            p0, p1 = halves(wr * sr - wi * si, wr * si + wi * sr)
            ye = by_right(p0 + p1, tables, 0)
            yo = by_right(p0 - p1, tables, 1)
            re = lanes(ye[:, :HALF], yo[:, :HALF])
            im = lanes(ye[:, HALF:], yo[:, HALF:])
            far[m, 0] = by_left(rows(re[:HALF] + re[HALF:], im[:HALF] + im[HALF:]), tables, 2)
            far[m, 1] = by_left(rows(re[:HALF] - re[HALF:], im[:HALF] - im[HALF:]), tables, 3)
        amp = jnp.dot(sort_row, amps[p], preferred_element_type=f32).astype(bf16)
        amp = jnp.dot(amp, sort_col, preferred_element_type=f32)
        for e in range(2):
            power = 0.0
            for m in range(2):
                z = far[m, e]
                power = power + z[:HALF] * z[:HALF] + z[HALF:] * z[HALF:]
            factor = 1.0 - amp[e * HALF : (e + 1) * HALF] * jnp.minimum(lax.rsqrt(power), 1.0 / floor_level)
            factor = rows(factor, factor)
            for m in range(2):
                far[m, e] = far[m, e] * factor
        for m in range(2):
            u = by_left(far[m, 0], tables, 4)
            v = by_left(far[m, 1], tables, 5)
            s, d = u + v, u - v
            re = rows(s[:HALF], d[:HALF])
            im = rows(s[HALF:], d[HALF:])
            ie, io = halves(re, im)
            u = by_right(ie, tables, 6)
            v = by_right(io, tables, 7)
            s, d = u + v, u - v
            cr = lanes(s[:, :HALF], d[:, :HALF])
            ci = lanes(s[:, HALF:], d[:, HALF:])
            sr, si = patch[2], patch[3]
            wr, wi = waves[p, 0, m].astype(f32), waves[p, 1, m].astype(f32)
            gr, gi = wr * cr + wi * ci, wr * ci - wi * cr
            if m == 0:
                upd[2], upd[3] = gr, gi
            else:
                upd[2], upd[3] = upd[2] + gr, upd[3] + gi
            p0, p1 = halves(sr * cr + si * ci, sr * ci - si * cr)
            u = by_right(p0 + p1, tables, 8)
            v = by_right(p0 - p1, tables, 9)
            s, d = u + v, u - v
            re = lanes(s[:, :HALF], d[:, :HALF])
            im = lanes(s[:, HALF:], d[:, HALF:])
            u = by_left(rows(re[:HALF] + re[HALF:], im[:HALF] + im[HALF:]), tables, 10)
            v = by_left(rows(re[:HALF] - re[HALF:], im[:HALF] - im[HALF:]), tables, 11)
            s, d = u + v, u - v
            br = rows(s[:HALF], d[:HALF])
            bi = rows(s[HALF:], d[HALF:])
            pr, pi = probe[0, m], probe[1, m]
            gr, gi = pr * br + pi * bi, pr * bi - pi * br
            if m == 0:
                upd[0], upd[1] = gr, gi
            else:
                upd[0], upd[1] = upd[0] + gr, upd[1] + gi
            ar, ai = patch[0], patch[1]
            grad_probe[0, m] = grad_probe[0, m] + (ar * br + ai * bi)
            grad_probe[1, m] = grad_probe[1, m] + (ar * bi - ai * br)
        for c in range(4):
            high, low = split(upd[c])
            moved = jnp.dot(lanes(high, low), rows(place, place), preferred_element_type=f32)
            moved = rows(moved, jnp.zeros((TALL - PX, 3 * HALF), f32))
            moved = pltpu.roll(moved, row_rest, 0)
            grad[c, pl.ds(row_base, TALL), :] = grad[c, pl.ds(row_base, TALL), :] + moved
        return carry

    lax.fori_loop(0, row_ref.shape[0], visit, 0)
    left_rim[...] = grad[:, :512, :HALF]
    own[...] = grad[:, :512, HALF : 2 * HALF]
    right_rim[...] = grad[:, :512, 2 * HALF :]


def compute(mid_obj, left_obj, right_obj, probe, waves, amps, row_at, col_at):
    tables = jnp.asarray(transform_tables())
    strip = jax.ShapeDtypeStruct(mid_obj.shape, f32)
    vmem = pl.BlockSpec(memory_space=pltpu.VMEM)
    smem = pl.BlockSpec(memory_space=pltpu.SMEM)
    return pl.pallas_call(
        compute_kernel,
        out_shape=[strip, strip, strip, jax.ShapeDtypeStruct((2, 2, PX, PX), f32)],
        in_specs=[smem, smem] + [vmem] * 7,
        out_specs=[vmem] * 4,
        scratch_shapes=[
            pltpu.VMEM((4, 520, 3 * HALF), f32),
            pltpu.VMEM((4, 520, 3 * HALF), f32),
            pltpu.VMEM((4, PX, PX), f32),
            pltpu.VMEM((2, 2, PX, PX), f32),
            pltpu.VMEM((4, PX, PX), f32),
        ],
        compiler_params=pltpu.CompilerParams(vmem_limit_bytes=60 * 1024 * 1024),
        name="gradient",
    )(row_at, col_at, mid_obj, left_obj, right_obj, probe, waves, amps, tables)


def exchange_kernel(own, left_rim, right_rim, probe_sum, total_out, shard_out, squares_out,
                    from_right, from_left, pieces, r1, s1, r2, s2, r3, s3, r4, fin, q1, q2,
                    rim_sems, pair_sems, sems3, sems4, sems5, sems6, sems7):
    g = lax.axis_index("group")
    t = lax.axis_index("tile")
    layer, core = g // 2, g % 2
    x, zy = t // 16, t % 16
    spot = x * 4 + g
    right = (g, (t + 1) % 64)
    left = (g, (t + 63) % 64)
    other_core = (layer * 2 + 1 - core, t)
    other_layer = ((1 - layer) * 2 + core, t)

    def along_x(j):
        return (g, (x + j) % 4 * 16 + zy)

    def along_zy(j):
        return (g, x * 16 + (zy + j) % 16)

    def along_group(j):
        return ((g + j) % 4, t)

    def along_spot(j):
        to = (spot + j) % 16
        return (to % 4, to // 4 * 16 + zy)

    barrier = pltpu.get_barrier_semaphore()
    partners = [right, left] + [along_zy(j) for j in range(1, 16)] + [along_spot(j) for j in range(1, 16)]
    for partner in partners:
        pl.semaphore_signal(barrier, inc=1, device_id=partner, device_id_type=pl.DeviceIdType.MESH)
    pl.semaphore_wait(barrier, len(partners))

    def send(src, dst, sems, device):
        copy = pltpu.make_async_remote_copy(
            src_ref=src, dst_ref=dst, send_sem=sems.at[0], recv_sem=sems.at[1],
            device_id=device, device_id_type=pl.DeviceIdType.MESH,
        )
        copy.start()
        return copy

    rim_copies = [
        send(left_rim, from_right, rim_sems.at[0], left),
        send(right_rim, from_left, rim_sems.at[1], right),
    ]
    for h in range(2):
        pieces[h] = probe_sum[:, h * HALF : (h + 1) * HALF].reshape(64, 2, 8, HALF)
    copy = send(pieces.at[1 - core], r1, pair_sems.at[0], other_core)
    copy.wait()
    for l in range(2):
        s1[l] = pieces[core, :, l] + r1[:, l]
    copy = send(s1.at[1 - layer], r2, pair_sems.at[1], other_layer)
    copy.wait()
    s2[...] = s1[layer] + r2[...]
    copies = []
    for j in range(1, 4):
        away = pl.multiple_of((x + j) % 4 * 16, 16)
        copies.append(send(s2.at[pl.ds(away, 16)], r3.at[j - 1], sems3.at[j - 1], along_x(j)))
    for copy in copies:
        copy.wait()
    s3[...] = s2[pl.ds(pl.multiple_of(x * 16, 16), 16)] + r3[0] + r3[1] + r3[2]
    copies = []
    for j in range(1, 16):
        copies.append(send(s3.at[(zy + j) % 16], r4.at[j - 1], sems4.at[j - 1], along_zy(j)))
    for copy in copies:
        copy.wait()
    piece = s3[zy]
    for j in range(15):
        piece = piece + r4[j]
    fin[0] = piece
    gathers = [send(fin.at[0], fin.at[j], sems5.at[j - 1], along_group(j)) for j in range(1, 4)]
    for copy in rim_copies:
        copy.wait()
    with_right = jnp.where(t < 63, 1.0, 0.0)
    with_left = jnp.where(t > 0, 1.0, 0.0)
    acc = jnp.zeros((8, HALF), f32)
    for c in range(4):
        total = own[c] + from_right[c] * with_right + from_left[c] * with_left
        total_out[c] = total
        acc = acc + jnp.sum((total * total).reshape(64, 8, HALF), axis=0)
    object_row = jnp.sum(acc, axis=0, keepdims=True)
    probe_row = jnp.sum(piece * piece, axis=0, keepdims=True)
    top = lax.broadcasted_iota(jnp.int32, (8, HALF), 0) < 4
    q1[0] = jnp.where(top, object_row, probe_row)
    copies = [send(q1.at[0], q1.at[j], sems6.at[j - 1], along_zy(j)) for j in range(1, 16)]
    for copy in copies:
        copy.wait()
    both = q1[zy]
    for s in range(1, 16):
        both = both + q1[(zy + 16 - s) % 16]
    q2[0] = both
    copies = [send(q2.at[0], q2.at[j], sems7.at[j - 1], along_spot(j)) for j in range(1, 16)]
    for copy in copies:
        copy.wait()
    both = q2[spot]
    for s in range(1, 16):
        both = both + q2[(spot + 16 - s) % 16]
    squares_out[...] = both
    for copy in gathers:
        copy.wait()
    for s in range(4):
        shard_out[s // 2 * 8 : s // 2 * 8 + 8, s % 2 * HALF : s % 2 * HALF + HALF] = fin[(g + 4 - s) % 4]


def exchange(own, left_rim, right_rim, probe_sum):
    strip = own.shape
    tile = (8, HALF)
    vmem = pl.BlockSpec(memory_space=pltpu.VMEM)
    sem = pltpu.SemaphoreType.DMA
    return pl.pallas_call(
        exchange_kernel,
        out_shape=[
            jax.ShapeDtypeStruct(strip, f32),
            jax.ShapeDtypeStruct((16, PX), f32),
            jax.ShapeDtypeStruct(tile, f32),
        ],
        in_specs=[vmem] * 4,
        out_specs=[vmem] * 3,
        scratch_shapes=[
            pltpu.VMEM(strip, f32),
            pltpu.VMEM(strip, f32),
            pltpu.VMEM((2, 64, 2, *tile), f32),
            pltpu.VMEM((64, 2, *tile), f32),
            pltpu.VMEM((2, 64, *tile), f32),
            pltpu.VMEM((64, *tile), f32),
            pltpu.VMEM((64, *tile), f32),
            pltpu.VMEM((3, 16, *tile), f32),
            pltpu.VMEM((16, *tile), f32),
            pltpu.VMEM((15, *tile), f32),
            pltpu.VMEM((4, *tile), f32),
            pltpu.VMEM((16, *tile), f32),
            pltpu.VMEM((16, *tile), f32),
            sem((2, 2)), sem((2, 2)), sem((3, 2)), sem((15, 2)), sem((3, 2)), sem((15, 2)), sem((15, 2)),
        ],
        compiler_params=pltpu.CompilerParams(
            collective_id=0, has_side_effects=True, vmem_limit_bytes=40 * 1024 * 1024
        ),
        name="exchange",
    )(own, left_rim, right_rim, probe_sum)


def shards(object_slices, probe, mid_waves, amplitudes, row_offsets, col_offsets):
    count = lax.axis_size("tile")
    left = lax.ppermute(object_slices, "tile", [(i, i + 1) for i in range(count - 1)])
    right = lax.ppermute(object_slices, "tile", [(i + 1, i) for i in range(count - 1)])
    own, left_rim, right_rim, grad_probe = compute(
        object_slices, left, right, probe.reshape(2, 2, PX, PX), mid_waves[0, 0], amplitudes[0, 0],
        row_offsets[0, 0], col_offsets[0, 0],
    )
    total, shard, squares = exchange(own, left_rim, right_rim, grad_probe.reshape(4 * PX, PX))
    object_mean = jnp.sum(squares[0]) / (4 * object_slices.shape[1] * object_slices.shape[2] * 256)
    probe_mean = jnp.sum(squares[4]) / (4 * PX * PX)
    object_new = object_slices.astype(f32) - total * (object_step / jnp.sqrt(object_mean + epsilon))
    start = lax.axis_index("tile") * 16
    probe_rows = lax.dynamic_slice_in_dim(probe, start, 16, 0)
    probe_new = probe_rows - shard * (probe_step / jnp.sqrt(probe_mean + epsilon))
    return (object_new, probe_new)


def solution(mesh):
    return jax.shard_map(
        shards,
        mesh=mesh,
        in_specs=(
            P(None, "group", "tile"),
            P(),
            P("group", "tile", None, None, None, None, None),
            P("group", "tile", None, None, None),
            P("group", "tile", None),
            P("group", "tile", None),
        ),
        out_specs=(P(None, "group", "tile"), P("tile", None)),
        check_vma=False,
    )
```

```python
import numpy as np
import ml_dtypes
import jax
import jax.numpy as jnp
from jax import lax
from jax.sharding import PartitionSpec as P
from jax.experimental import pallas as pl
from jax.experimental.pallas import tpu as pltpu

phase_rate = 0.25
floor_level = 0.5
object_step = 0.5
probe_step = 0.5
epsilon = 1e-06
f32 = jnp.float32
bf16 = jnp.bfloat16
PX = 256
HALF = 128
TALL = PX + 8
ROWS = 512
POSITIONS = 3
CHUNKS = 8
LEVELS = 32767.0
OBJECT_COUNT = 4 * 2048 * 8192
PROBE_COUNT = 4 * PX * PX


def right_form(m):
    return np.block([[m.real, m.imag], [-m.imag, m.real]])


def left_form(m):
    return np.block([[m.real, -m.imag], [m.imag, m.real]])


def transform_tables():
    n = np.arange(HALF)[:, None]
    k = np.arange(HALF)[None, :]
    root = -2j * np.pi / PX
    even = np.exp(root * ((2 * n * k) % PX)) / np.sqrt(PX)
    odd = np.exp(root * ((n * (2 * k + 1)) % PX)) / np.sqrt(PX)
    freq = np.arange(PX)
    freq = np.where(freq < HALF, freq, freq - PX)
    phase = np.exp(2j * np.pi * phase_rate * freq * freq / PX)
    ring = np.fft.ifft(phase)
    i, j = np.meshgrid(np.arange(HALF), np.arange(HALF), indexing="ij")
    near, far = ring[(i - j) % PX], ring[(i - j + HALF) % PX]
    plus, minus = (near + far) / 2, (near - far) / 2
    forms = [
        right_form(even), right_form(odd),
        left_form(even.T), left_form(odd.T),
        left_form(even.conj()), left_form(odd.conj()),
        right_form(even.conj().T), right_form(odd.conj().T),
        right_form(plus.T), right_form(minus.T),
        left_form(plus), left_form(minus),
    ]
    whole = np.stack(forms)
    high = whole.astype(ml_dtypes.bfloat16)
    low = (whole - high.astype(np.float64)).astype(ml_dtypes.bfloat16)
    return np.stack([high, low], axis=1)


def split(x):
    high = x.astype(bf16)
    return high, (x - high.astype(f32)).astype(bf16)


def by_right(x, tables, index):
    high, low = split(x)
    t = tables[index, 0]
    return jnp.dot(
        jnp.concatenate([high, low, high], axis=1),
        jnp.concatenate([t, t, tables[index, 1]], axis=0),
        preferred_element_type=f32,
    )


def by_left(x, tables, index):
    high, low = split(x)
    t = tables[index, 0]
    return jnp.dot(
        jnp.concatenate([t, t, tables[index, 1]], axis=1),
        jnp.concatenate([high, low, high], axis=0),
        preferred_element_type=f32,
    )


def lanes(a, b):
    return jnp.concatenate([a, b], axis=1)


def rows(a, b):
    return jnp.concatenate([a, b], axis=0)


def halves(re, im):
    return lanes(re[:, :HALF], im[:, :HALF]), lanes(re[:, HALF:], im[:, HALF:])


def quantised(values, codes, scales):
    for k in range(CHUNKS):
        part = values[k * 64 : (k + 1) * 64]
        top = jnp.maximum(jnp.max(jnp.abs(part), axis=0, keepdims=True), 1e-30)
        scales[k : k + 1] = top * (1.0 / LEVELS)
        codes[k * 64 : (k + 1) * 64] = jnp.round(part * (LEVELS / top)).astype(jnp.int32).astype(jnp.int16)


def restored(codes, scales, k):
    return codes[k * 64 : (k + 1) * 64].astype(jnp.int32).astype(f32) * scales[k : k + 1]


def kernel(row_ref, col_ref, own_obj, probe_hbm, waves_hbm, amps_hbm, tables_hbm,
           object_new, probe_new,
           probe, waves, amps, tables, halo, obj, grad, pad, patch, far, back, upd, sorted_amps, gp,
           out_codes, out_scales, in_codes, in_scales,
           r1, s1, r2, s2, r3, s3, r4, fin, q1, q2,
           load_sems, halo_sems, code_sems, scale_sems, pair_sems, sems3, sems4, sems5, sems6, sems7):
    g = lax.axis_index("group")
    t = lax.axis_index("tile")
    layer, core = g // 2, g % 2
    x, zy = t // 16, t % 16
    spot = x * 4 + g
    right = (g, (t + 1) % 64)
    left = (g, (t + 63) % 64)
    other_core = (layer * 2 + 1 - core, t)
    other_layer = ((1 - layer) * 2 + core, t)

    def along_x(j):
        return (g, (x + j) % 4 * 16 + zy)

    def along_zy(j):
        return (g, x * 16 + (zy + j) % 16)

    def along_group(j):
        return ((g + j) % 4, t)

    def along_spot(j):
        to = (spot + j) % 16
        return (to % 4, to // 4 * 16 + zy)

    loads = [
        pltpu.make_async_copy(src, dst, load_sems.at[i])
        for i, (src, dst) in enumerate(
            [(amps_hbm, amps), (waves_hbm, waves), (tables_hbm, tables), (probe_hbm, probe)]
        )
    ]
    for load in loads:
        load.start()
    barrier = pltpu.get_barrier_semaphore()
    partners = [right, left] + [along_zy(j) for j in range(1, 16)] + [along_spot(j) for j in range(1, 16)]
    for partner in partners:
        pl.semaphore_signal(barrier, inc=1, device_id=partner, device_id_type=pl.DeviceIdType.MESH)
    pl.semaphore_wait(barrier, len(partners))

    def send(src, dst, sems, device):
        copy = pltpu.make_async_remote_copy(
            src_ref=src, dst_ref=dst, send_sem=sems.at[0], recv_sem=sems.at[1],
            device_id=device, device_id_type=pl.DeviceIdType.MESH,
        )
        copy.start()
        return copy

    halo_copies = []
    for s in (1, 0):
        part = pl.ds(2 * s, 2)
        halo_copies.append([
            send(own_obj.at[part], halo.at[0, part], halo_sems.at[0, s], right),
            send(own_obj.at[part], halo.at[1, part], halo_sems.at[1, s], left),
        ])

    at_row = lax.broadcasted_iota(jnp.int32, (PX, PX), 0)
    at_col = lax.broadcasted_iota(jnp.int32, (PX, PX), 1)
    sort_row = (at_col == jnp.where(at_row < HALF, 2 * at_row, 2 * at_row - PX + 1)).astype(f32).astype(bf16)
    sort_col = (at_row == jnp.where(at_col < HALF, 2 * at_col, 2 * at_col - PX + 1)).astype(f32).astype(bf16)
    grad[...] = jnp.zeros_like(grad)
    pad[:, :PX] = jnp.zeros((2, PX, 3 * HALF), f32)
    pad[:, PX + TALL :] = jnp.zeros((2, PX - 8, 3 * HALF), f32)
    obj[:, ROWS:, :] = jnp.zeros((2, 8, 3 * HALF), f32)
    gp[...] = jnp.zeros_like(gp)
    loads[0].wait()

    def sort_amps(p, carry):
        amp = jnp.dot(sort_row, amps[p], preferred_element_type=f32).astype(bf16)
        sorted_amps[p] = jnp.dot(amp, sort_col, preferred_element_type=f32)
        return carry

    lax.fori_loop(0, POSITIONS, sort_amps, 0)
    has_left = jnp.where(t > 0, 1.0, 0.0)
    has_right = jnp.where(t < 63, 1.0, 0.0)

    def widen(first):
        for c in range(2):
            obj[c, :ROWS, :HALF] = halo[0, first + c].astype(f32) * has_left
            obj[c, :ROWS, HALF : 2 * HALF] = own_obj[first + c].astype(f32)
            obj[c, :ROWS, 2 * HALF :] = halo[1, first + c].astype(f32) * has_right

    def offsets(p):
        row_at = row_ref[p]
        return lax.div(row_at, 8), lax.rem(row_at, 8), col_ref[p]

    def take_patch(p, dst):
        row_tile, row_rest, col_at = offsets(p)
        pick = (
            lax.broadcasted_iota(jnp.int32, (3 * HALF, PX), 0)
            == lax.broadcasted_iota(jnp.int32, (3 * HALF, PX), 1) + col_at
        ).astype(f32).astype(bf16)
        for c in range(2):
            raw = obj[c, pl.ds(row_tile * 8, TALL), :].astype(bf16)
            wide = jnp.dot(raw, pick, preferred_element_type=f32)
            dst[c] = pltpu.roll(wide, TALL - row_rest, 0)[:PX]

    def add_patch(p, first, values):
        row_tile, row_rest, col_at = offsets(p)
        place = (
            lax.broadcasted_iota(jnp.int32, (PX, 3 * HALF), 1)
            == lax.broadcasted_iota(jnp.int32, (PX, 3 * HALF), 0) + col_at
        ).astype(f32).astype(bf16)
        for c in range(2):
            high, low = split(values[c])
            moved = jnp.dot(lanes(high, low), rows(place, place), preferred_element_type=f32)
            moved = rows(moved, jnp.zeros((TALL - PX, 3 * HALF), f32))
            pad[c, PX : PX + TALL] = pltpu.roll(moved, row_rest, 0)
            grad[first + c] = grad[first + c] + pad[c, pl.ds((PX // 8 - row_tile) * 8, ROWS), :]

    def send_rims(first):
        copies = []
        for side, device in ((0, left), (1, right)):
            for c in range(2):
                quantised(
                    grad[first + c, :, side * 2 * HALF : side * 2 * HALF + HALF],
                    out_codes.at[side, first + c], out_scales.at[side, first + c],
                )
            part = pl.ds(first, 2)
            copies.append(send(out_codes.at[side, part], in_codes.at[side, part], code_sems.at[side, first // 2], device))
            copies.append(send(out_scales.at[side, part], in_scales.at[side, part], scale_sems.at[side, first // 2], device))
        return copies

    for load in loads[1:]:
        load.wait()
    for copy in halo_copies[0]:
        copy.wait()
    widen(2)

    def phase_one(p, carry):
        take_patch(p, patch)
        for m in range(2):
            sr, si = patch[0], patch[1]
            wr, wi = waves[p, 0, m].astype(f32), waves[p, 1, m].astype(f32)
            p0, p1 = halves(wr * sr - wi * si, wr * si + wi * sr)
            ye = by_right(p0 + p1, tables, 0)
            yo = by_right(p0 - p1, tables, 1)
            re = lanes(ye[:, :HALF], yo[:, :HALF])
            im = lanes(ye[:, HALF:], yo[:, HALF:])
            far[m, 0] = by_left(rows(re[:HALF] + re[HALF:], im[:HALF] + im[HALF:]), tables, 2)
            far[m, 1] = by_left(rows(re[:HALF] - re[HALF:], im[:HALF] - im[HALF:]), tables, 3)
        for e in range(2):
            power = 0.0
            for m in range(2):
                z = far[m, e]
                power = power + z[:HALF] * z[:HALF] + z[HALF:] * z[HALF:]
            factor = 1.0 - sorted_amps[p, e * HALF : (e + 1) * HALF] * jnp.minimum(
                lax.rsqrt(power), 1.0 / floor_level
            )
            factor = rows(factor, factor)
            for m in range(2):
                far[m, e] = far[m, e] * factor
        for m in range(2):
            u = by_left(far[m, 0], tables, 4)
            v = by_left(far[m, 1], tables, 5)
            s, d = u + v, u - v
            ie, io = halves(rows(s[:HALF], d[:HALF]), rows(s[HALF:], d[HALF:]))
            u = by_right(ie, tables, 6)
            v = by_right(io, tables, 7)
            s, d = u + v, u - v
            cr = lanes(s[:, :HALF], d[:, :HALF])
            ci = lanes(s[:, HALF:], d[:, HALF:])
            sr, si = patch[0], patch[1]
            wr, wi = waves[p, 0, m].astype(f32), waves[p, 1, m].astype(f32)
            gr, gi = wr * cr + wi * ci, wr * ci - wi * cr
            if m == 0:
                upd[p, 0], upd[p, 1] = gr, gi
            else:
                upd[p, 0], upd[p, 1] = upd[p, 0] + gr, upd[p, 1] + gi
            back[p, m, 0] = sr * cr + si * ci
            back[p, m, 1] = sr * ci - si * cr
        add_patch(p, 2, upd.at[p])
        return carry

    lax.fori_loop(0, POSITIONS, phase_one, 0)
    rim_two = send_rims(2)
    for copy in halo_copies[1]:
        copy.wait()
    widen(0)

    def phase_two(p, m):
        if m == 0:
            take_patch(p, upd.at[p])
        p0, p1 = halves(back[p, m, 0], back[p, m, 1])
        u = by_right(p0 + p1, tables, 8)
        v = by_right(p0 - p1, tables, 9)
        s, d = u + v, u - v
        re = lanes(s[:, :HALF], d[:, :HALF])
        im = lanes(s[:, HALF:], d[:, HALF:])
        u = by_left(rows(re[:HALF] + re[HALF:], im[:HALF] + im[HALF:]), tables, 10)
        v = by_left(rows(re[:HALF] - re[HALF:], im[:HALF] - im[HALF:]), tables, 11)
        s, d = u + v, u - v
        br = rows(s[:HALF], d[:HALF])
        bi = rows(s[HALF:], d[HALF:])
        pr, pi = probe[0, m], probe[1, m]
        ar, ai = upd[p, 0], upd[p, 1]
        gr, gi = pr * br + pi * bi, pr * bi - pi * br
        for part, value in enumerate((ar * br + ai * bi, ar * bi - ai * br)):
            for h in range(2):
                half = value[:, h * HALF : (h + 1) * HALF].reshape(16, 2, 8, HALF)
                gp[m, h, part] = gp[m, h, part] + half
        if m == 0:
            back[p, 0, 0], back[p, 0, 1] = gr, gi
        else:
            patch[0], patch[1] = back[p, 0, 0] + gr, back[p, 0, 1] + gi
            add_patch(p, 0, patch)

    def first_mode(p, carry):
        phase_two(p, 0)
        return carry

    def second_mode(p, carry):
        phase_two(p, 1)
        return carry

    def stage_one(m):
        return [send(gp.at[m, 1 - core], r1.at[m], pair_sems.at[0, m], other_core)]

    def stage_two(m):
        for l in range(2):
            s1[m, l] = gp[m, core, :, :, l] + r1[m, :, :, l]
        return [send(s1.at[m, 1 - layer], r2.at[m], pair_sems.at[1, m], other_layer)]

    def finish(copies):
        for copy in copies:
            copy.wait()

    lax.fori_loop(0, POSITIONS, first_mode, 0)
    one_a = stage_one(0)
    lax.fori_loop(0, 1, second_mode, 0)
    finish(one_a)
    two_a = stage_two(0)
    lax.fori_loop(1, POSITIONS, second_mode, 0)
    one_b = stage_one(1)
    rim_one = send_rims(0)
    finish(two_a)
    finish(one_b)
    two_b = stage_two(1)
    finish(rim_two)
    acc = jnp.zeros((8, HALF), f32)

    def total_of(c, acc):
        for k in range(CHUNKS):
            part = pl.ds(k * 64, 64)
            total = grad[c, part, HALF : 2 * HALF]
            total = total + restored(in_codes.at[0, c], in_scales.at[0, c], k) * has_right
            total = total + restored(in_codes.at[1, c], in_scales.at[1, c], k) * has_left
            object_new[c, part] = total
            acc = acc + jnp.sum((total * total).reshape(8, 8, HALF), axis=0)
        return acc

    for c in (2, 3):
        acc = total_of(c, acc)
    finish(two_b)
    for m in range(2):
        for part in range(2):
            s2[part * 2 + m] = s1[m, layer, part] + r2[m, part]
    copies = []
    for j in range(1, 4):
        copies.append(send(s2.at[(x + j) % 4], r3.at[j - 1], sems3.at[j - 1], along_x(j)))
    finish(copies)
    s3[...] = s2[x] + r3[0] + r3[1] + r3[2]
    four = [send(s3.at[(zy + j) % 16], r4.at[j - 1], sems4.at[j - 1], along_zy(j)) for j in range(1, 16)]
    finish(rim_one)
    for c in (0, 1):
        acc = total_of(c, acc)
    finish(four)
    piece = s3[zy]
    for j in range(15):
        piece = piece + r4[j]
    fin[0] = piece
    gathers = [send(fin.at[0], fin.at[j], sems5.at[j - 1], along_group(j)) for j in range(1, 4)]
    object_row = jnp.sum(acc, axis=0, keepdims=True)
    probe_row = jnp.sum(piece * piece, axis=0, keepdims=True)
    top = lax.broadcasted_iota(jnp.int32, (8, HALF), 0) < 4
    q1[0] = jnp.where(top, object_row, probe_row)
    finish([send(q1.at[0], q1.at[j], sems6.at[j - 1], along_zy(j)) for j in range(1, 16)])
    both = q1[zy]
    for s in range(1, 16):
        both = both + q1[(zy + 16 - s) % 16]
    q2[0] = both
    finish([send(q2.at[0], q2.at[j], sems7.at[j - 1], along_spot(j)) for j in range(1, 16)])
    both = q2[spot]
    for s in range(1, 16):
        both = both + q2[(spot + 16 - s) % 16]
    squares = jnp.sum(both, axis=1, keepdims=True)
    object_step_size = object_step * lax.rsqrt(squares[0:1] * (1.0 / OBJECT_COUNT) + epsilon)
    probe_step_size = probe_step * lax.rsqrt(squares[4:5] * (1.0 / PROBE_COUNT) + epsilon)
    for c in range(4):
        object_new[c] = own_obj[c].astype(f32) - object_new[c] * object_step_size
    finish(gathers)
    old = probe.at[x // 2, x % 2]
    for s in range(4):
        part = old[pl.ds(pl.multiple_of(zy * 16 + s // 2 * 8, 8), 8), s % 2 * HALF : s % 2 * HALF + HALF]
        probe_new[s // 2 * 8 : s // 2 * 8 + 8, s % 2 * HALF : s % 2 * HALF + HALF] = (
            part - fin[(g + 4 - s) % 4] * probe_step_size
        )


def shards(object_slices, probe, mid_waves, amplitudes, row_offsets, col_offsets):
    tables = jnp.asarray(transform_tables())
    tile = (8, HALF)
    whole = (PX, PX)
    vmem = pl.BlockSpec(memory_space=pltpu.VMEM)
    smem = pl.BlockSpec(memory_space=pltpu.SMEM)
    anywhere = pl.BlockSpec(memory_space=pl.ANY)
    sem = pltpu.SemaphoreType.DMA
    return pl.pallas_call(
        kernel,
        out_shape=[
            jax.ShapeDtypeStruct(object_slices.shape, f32),
            jax.ShapeDtypeStruct((16, PX), f32),
        ],
        in_specs=[smem, smem, vmem] + [anywhere] * 4,
        out_specs=[vmem] * 2,
        scratch_shapes=[
            pltpu.VMEM((2, 2, *whole), f32),
            pltpu.VMEM((3, 2, 2, *whole), bf16),
            pltpu.VMEM((3, *whole), bf16),
            pltpu.VMEM(tables.shape, bf16),
            pltpu.VMEM((2, 4, ROWS, HALF), bf16),
            pltpu.VMEM((2, ROWS + 8, 3 * HALF), f32),
            pltpu.VMEM((4, ROWS, 3 * HALF), f32),
            pltpu.VMEM((2, ROWS + PX, 3 * HALF), f32),
            pltpu.VMEM((2, *whole), f32),
            pltpu.VMEM((2, 2, *whole), f32),
            pltpu.VMEM((3, 2, 2, *whole), f32),
            pltpu.VMEM((3, 2, *whole), f32),
            pltpu.VMEM((3, *whole), f32),
            pltpu.VMEM((2, 2, 2, 16, 2, *tile), f32),
            pltpu.VMEM((2, 4, ROWS, HALF), jnp.int16),
            pltpu.VMEM((2, 4, *tile), f32),
            pltpu.VMEM((2, 4, ROWS, HALF), jnp.int16),
            pltpu.VMEM((2, 4, *tile), f32),
            pltpu.VMEM((2, 2, 16, 2, *tile), f32),
            pltpu.VMEM((2, 2, 2, 16, *tile), f32),
            pltpu.VMEM((2, 2, 16, *tile), f32),
            pltpu.VMEM((4, 16, *tile), f32),
            pltpu.VMEM((3, 16, *tile), f32),
            pltpu.VMEM((16, *tile), f32),
            pltpu.VMEM((15, *tile), f32),
            pltpu.VMEM((4, *tile), f32),
            pltpu.VMEM((16, *tile), f32),
            pltpu.VMEM((16, *tile), f32),
            sem((4,)), sem((2, 2, 2)), sem((2, 2, 2)), sem((2, 2, 2)), sem((2, 2, 2)),
            sem((3, 2)), sem((15, 2)), sem((3, 2)), sem((15, 2)), sem((15, 2)),
        ],
        compiler_params=pltpu.CompilerParams(
            collective_id=0, has_side_effects=True, vmem_limit_bytes=56 * 1024 * 1024
        ),
        name="update",
    )(
        row_offsets[0, 0], col_offsets[0, 0], object_slices, probe.reshape(2, 2, *whole),
        mid_waves[0, 0], amplitudes[0, 0], tables,
    )


def solution(mesh):
    return jax.shard_map(
        shards,
        mesh=mesh,
        in_specs=(
            P(None, "group", "tile"),
            P(),
            P("group", "tile", None, None, None, None, None),
            P("group", "tile", None, None, None),
            P("group", "tile", None),
            P("group", "tile", None),
        ),
        out_specs=(P(None, "group", "tile"), P("tile", None)),
        check_vma=False,
    )
```

```python
import numpy as np
import ml_dtypes
import jax
import jax.numpy as jnp
from jax import lax
from jax.sharding import PartitionSpec as P
from jax.experimental import pallas as pl
from jax.experimental.pallas import tpu as pltpu

phase_rate = 0.25
floor_level = 0.5
object_step = 0.5
probe_step = 0.5
epsilon = 1e-06
f32 = jnp.float32
bf16 = jnp.bfloat16
PX = 256
HALF = 128
TALL = PX + 8
ROWS = 512
POSITIONS = 3
CHUNKS = 8
PIECES = 4
CHUNK_ROWS = ROWS // PIECES
LEVELS = 32767.0
OBJECT_COUNT = 4 * 2048 * 8192
PROBE_COUNT = 4 * PX * PX


def right_form(m):
    return np.block([[m.real, m.imag], [-m.imag, m.real]])


def left_form(m):
    return np.block([[m.real, -m.imag], [m.imag, m.real]])


def transform_tables():
    n = np.arange(HALF)[:, None]
    k = np.arange(HALF)[None, :]
    root = -2j * np.pi / PX
    even = np.exp(root * ((2 * n * k) % PX)) / np.sqrt(PX)
    odd = np.exp(root * ((n * (2 * k + 1)) % PX)) / np.sqrt(PX)
    freq = np.arange(PX)
    freq = np.where(freq < HALF, freq, freq - PX)
    phase = np.exp(2j * np.pi * phase_rate * freq * freq / PX)
    ring = np.fft.ifft(phase)
    i, j = np.meshgrid(np.arange(HALF), np.arange(HALF), indexing="ij")
    near, far = ring[(i - j) % PX], ring[(i - j + HALF) % PX]
    plus, minus = (near + far) / 2, (near - far) / 2
    forms = [
        right_form(even), right_form(odd),
        left_form(even.T), left_form(odd.T),
        left_form(even.conj()), left_form(odd.conj()),
        right_form(even.conj().T), right_form(odd.conj().T),
        right_form(plus.T), right_form(minus.T),
        left_form(plus), left_form(minus),
    ]
    whole = np.stack(forms)
    high = whole.astype(ml_dtypes.bfloat16)
    low = (whole - high.astype(np.float64)).astype(ml_dtypes.bfloat16)
    return np.stack([high, low], axis=1)


def split(x):
    high = x.astype(bf16)
    return high, (x - high.astype(f32)).astype(bf16)


def by_right(x, tables, index):
    high, low = split(x)
    t = tables[index, 0]
    return jnp.dot(
        jnp.concatenate([high, low, high], axis=1),
        jnp.concatenate([t, t, tables[index, 1]], axis=0),
        preferred_element_type=f32,
    )


def by_left(x, tables, index):
    high, low = split(x)
    t = tables[index, 0]
    return jnp.dot(
        jnp.concatenate([t, t, tables[index, 1]], axis=1),
        jnp.concatenate([high, low, high], axis=0),
        preferred_element_type=f32,
    )


def lanes(a, b):
    return jnp.concatenate([a, b], axis=1)


def rows(a, b):
    return jnp.concatenate([a, b], axis=0)


def halves(re, im):
    return lanes(re[:, :HALF], im[:, :HALF]), lanes(re[:, HALF:], im[:, HALF:])


def quantised(values, codes, scales):
    for k in range(CHUNKS):
        part = values[k * 64 : (k + 1) * 64]
        top = jnp.maximum(jnp.max(jnp.abs(part), axis=0, keepdims=True), 1e-30)
        scales[k : k + 1] = top * (1.0 / LEVELS)
        codes[k * 64 : (k + 1) * 64] = jnp.round(part * (LEVELS / top)).astype(jnp.int32).astype(jnp.int16)


def restored(codes, scales, k):
    return codes[k * 64 : (k + 1) * 64].astype(jnp.int32).astype(f32) * scales[k : k + 1]


def kernel(row_ref, col_ref, own_obj, probe_hbm, waves_hbm, amps_hbm, tables_hbm,
           total_out, squares_out, shard_out,
           probe, waves, amps, tables, halo, obj, grad, pad, patch, far, back, upd, sorted_amps, gp,
           out_codes, out_scales, in_codes, in_scales,
           halo_relay, code_relay, r1, s1, r2, s2, r3, s3, r4, fin, q1, q2,
           load_sems, direct_sems, chunk_sems, relay_sems, onward_sems, scale_sems, pair_sems,
           sems3, sems4, sems5, sems6, sems7):
    g = lax.axis_index("group")
    t = lax.axis_index("tile")
    layer, core = g // 2, g % 2
    x, zy = t // 16, t % 16
    spot = x * 4 + g
    right = (g, (t + 1) % 64)
    left = (g, (t + 63) % 64)
    y = zy % 4
    onward = ((g, (t + 4) % 64), (g, (t + 60) % 64))
    wrapped = ((g, t - y), (g, t - y + 3))
    at_end = (y == 3, y == 0)
    at_start = (y == 0, y == 3)
    other_core = (layer * 2 + 1 - core, t)
    other_layer = ((1 - layer) * 2 + core, t)

    def along_x(j):
        return (g, (x + j) % 4 * 16 + zy)

    def along_zy(j):
        return (g, x * 16 + (zy + j) % 16)

    def along_group(j):
        return ((g + j) % 4, t)

    def along_spot(j):
        to = (spot + j) % 16
        return (to % 4, to // 4 * 16 + zy)

    loads = [
        pltpu.make_async_copy(src, dst, load_sems.at[i])
        for i, (src, dst) in enumerate(
            [(amps_hbm, amps), (waves_hbm, waves), (tables_hbm, tables), (probe_hbm, probe)]
        )
    ]
    for load in loads:
        load.start()
    barrier = pltpu.get_barrier_semaphore()
    partners = [right, left, *onward] + [along_zy(j) for j in range(1, 16)] + [along_spot(j) for j in range(1, 16)]
    for partner in partners:
        pl.semaphore_signal(barrier, inc=1, device_id=partner, device_id_type=pl.DeviceIdType.MESH)
    pl.semaphore_wait(barrier, len(partners))

    def send(src, dst, sems, device):
        copy = pltpu.make_async_remote_copy(
            src_ref=src, dst_ref=dst, send_sem=sems.at[0], recv_sem=sems.at[1],
            device_id=device, device_id_type=pl.DeviceIdType.MESH,
        )
        copy.start()
        return copy

    class Swap:
        def __init__(self, number, src, dst, relay, first):
            self.number, self.src, self.dst, self.relay, self.first = number, src, dst, relay, first

        def near(self, side):
            return right if side == 0 else left

        def chunk(self, ref, k):
            return ref.at[pl.ds(k * CHUNK_ROWS, CHUNK_ROWS)]

        def copy(self, src, dst, send_sem, recv_sem, device):
            return pltpu.make_async_remote_copy(
                src_ref=src, dst_ref=dst, send_sem=send_sem, recv_sem=recv_sem,
                device_id=device, device_id_type=pl.DeviceIdType.MESH,
            )

        def direct(self, side):
            sems = direct_sems.at[self.number, side]
            return self.copy(
                self.src(side).at[self.first], self.dst(side).at[self.first], sems.at[0], sems.at[1], self.near(side)
            )

        def plain(self, side, k):
            sems = chunk_sems.at[self.number, side, k]
            second = self.first + 1
            return self.copy(
                self.chunk(self.src(side).at[second], k), self.chunk(self.dst(side).at[second], k),
                sems.at[0], sems.at[1], self.near(side),
            )

        def detour(self, side, k):
            sems = relay_sems.at[self.number, side, k]
            return self.copy(
                self.chunk(self.src(side).at[self.first + 1], k), self.chunk(self.relay(side), k),
                sems.at[0], sems.at[1], wrapped[side],
            )

        def forwarded(self, side, k):
            return self.copy(
                self.chunk(self.relay(side), k), self.chunk(self.dst(side).at[self.first + 1], k),
                onward_sems.at[self.number, side, k], chunk_sems.at[self.number, side, k].at[1], onward[side],
            )

        def start(self):
            for side in range(2):
                @pl.when(at_end[side])
                def _():
                    for k in range(PIECES):
                        self.detour(side, k).start()

                @pl.when(jnp.logical_not(at_end[side]))
                def _():
                    for k in range(PIECES):
                        self.plain(side, k).start()

            for side in range(2):
                self.direct(side).start()

        def forward(self):
            for side in range(2):
                @pl.when(at_start[side])
                def _():
                    for k in range(PIECES):
                        self.detour(side, k).wait_recv()
                        self.forwarded(side, k).start()

        def wait(self):
            for side in range(2):
                for k in range(PIECES):
                    self.plain(side, k).wait_recv()
                self.direct(side).wait()

                @pl.when(at_end[side])
                def _():
                    for k in range(PIECES):
                        self.detour(side, k).wait_send()

                @pl.when(jnp.logical_not(at_end[side]))
                def _():
                    for k in range(PIECES):
                        self.plain(side, k).wait_send()

                @pl.when(at_start[side])
                def _():
                    for k in range(PIECES):
                        self.forwarded(side, k).wait_send()

    def halo_swap(number, first):
        return Swap(number, lambda side: own_obj, lambda side: halo.at[side], lambda side: halo_relay.at[number, side], first)

    def rim_swap(number, first):
        return Swap(
            number, lambda side: out_codes.at[side], lambda side: in_codes.at[side],
            lambda side: code_relay.at[number - 2, side], first,
        )

    halo_two, halo_one = halo_swap(0, 2), halo_swap(1, 0)
    rim_two, rim_one = rim_swap(2, 2), rim_swap(3, 0)
    halo_two.start()
    halo_one.start()

    at_row = lax.broadcasted_iota(jnp.int32, (PX, PX), 0)
    at_col = lax.broadcasted_iota(jnp.int32, (PX, PX), 1)
    sort_row = (at_col == jnp.where(at_row < HALF, 2 * at_row, 2 * at_row - PX + 1)).astype(f32).astype(bf16)
    sort_col = (at_row == jnp.where(at_col < HALF, 2 * at_col, 2 * at_col - PX + 1)).astype(f32).astype(bf16)
    grad[...] = jnp.zeros_like(grad)
    pad[:, :PX] = jnp.zeros((2, PX, 3 * HALF), f32)
    pad[:, PX + TALL :] = jnp.zeros((2, PX - 8, 3 * HALF), f32)
    obj[:, ROWS:, :] = jnp.zeros((2, 8, 3 * HALF), f32)
    gp[...] = jnp.zeros_like(gp)
    loads[0].wait()

    def sort_amps(p, carry):
        amp = jnp.dot(sort_row, amps[p], preferred_element_type=f32).astype(bf16)
        sorted_amps[p] = jnp.dot(amp, sort_col, preferred_element_type=f32)
        return carry

    lax.fori_loop(0, POSITIONS, sort_amps, 0)
    has_left = jnp.where(t > 0, 1.0, 0.0)
    has_right = jnp.where(t < 63, 1.0, 0.0)

    def widen(first):
        for c in range(2):
            obj[c, :ROWS, :HALF] = halo[0, first + c].astype(f32) * has_left
            obj[c, :ROWS, HALF : 2 * HALF] = own_obj[first + c].astype(f32)
            obj[c, :ROWS, 2 * HALF :] = halo[1, first + c].astype(f32) * has_right

    def offsets(p):
        row_at = row_ref[p]
        return lax.div(row_at, 8), lax.rem(row_at, 8), col_ref[p]

    def take_patch(p, dst):
        row_tile, row_rest, col_at = offsets(p)
        pick = (
            lax.broadcasted_iota(jnp.int32, (3 * HALF, PX), 0)
            == lax.broadcasted_iota(jnp.int32, (3 * HALF, PX), 1) + col_at
        ).astype(f32).astype(bf16)
        for c in range(2):
            raw = obj[c, pl.ds(row_tile * 8, TALL), :].astype(bf16)
            wide = jnp.dot(raw, pick, preferred_element_type=f32)
            dst[c] = pltpu.roll(wide, TALL - row_rest, 0)[:PX]

    def add_patch(p, first, values):
        row_tile, row_rest, col_at = offsets(p)
        place = (
            lax.broadcasted_iota(jnp.int32, (PX, 3 * HALF), 1)
            == lax.broadcasted_iota(jnp.int32, (PX, 3 * HALF), 0) + col_at
        ).astype(f32).astype(bf16)
        for c in range(2):
            high, low = split(values[c])
            moved = jnp.dot(lanes(high, low), rows(place, place), preferred_element_type=f32)
            moved = rows(moved, jnp.zeros((TALL - PX, 3 * HALF), f32))
            pad[c, PX : PX + TALL] = pltpu.roll(moved, row_rest, 0)
            grad[first + c] = grad[first + c] + pad[c, pl.ds((PX // 8 - row_tile) * 8, ROWS), :]

    def send_rims(swap):
        first = swap.first
        copies = []
        for side in range(2):
            from_lane = 2 * HALF * (1 - side)
            for c in range(2):
                quantised(
                    grad[first + c, :, from_lane : from_lane + HALF],
                    out_codes.at[side, first + c], out_scales.at[side, first + c],
                )
        swap.start()
        for side in range(2):
            part = pl.ds(first, 2)
            copies.append(
                send(out_scales.at[side, part], in_scales.at[side, part], scale_sems.at[side, first // 2], swap.near(side))
            )
        return copies

    for load in loads[1:]:
        load.wait()
    halo_two.forward()
    halo_two.wait()
    widen(2)

    def phase_one(p, carry):
        take_patch(p, patch)
        for m in range(2):
            sr, si = patch[0], patch[1]
            wr, wi = waves[p, 0, m].astype(f32), waves[p, 1, m].astype(f32)
            p0, p1 = halves(wr * sr - wi * si, wr * si + wi * sr)
            ye = by_right(p0 + p1, tables, 0)
            yo = by_right(p0 - p1, tables, 1)
            re = lanes(ye[:, :HALF], yo[:, :HALF])
            im = lanes(ye[:, HALF:], yo[:, HALF:])
            far[m, 0] = by_left(rows(re[:HALF] + re[HALF:], im[:HALF] + im[HALF:]), tables, 2)
            far[m, 1] = by_left(rows(re[:HALF] - re[HALF:], im[:HALF] - im[HALF:]), tables, 3)
        for e in range(2):
            power = 0.0
            for m in range(2):
                z = far[m, e]
                power = power + z[:HALF] * z[:HALF] + z[HALF:] * z[HALF:]
            factor = 1.0 - sorted_amps[p, e * HALF : (e + 1) * HALF] * jnp.minimum(
                lax.rsqrt(power), 1.0 / floor_level
            )
            factor = rows(factor, factor)
            for m in range(2):
                far[m, e] = far[m, e] * factor
        for m in range(2):
            u = by_left(far[m, 0], tables, 4)
            v = by_left(far[m, 1], tables, 5)
            s, d = u + v, u - v
            ie, io = halves(rows(s[:HALF], d[:HALF]), rows(s[HALF:], d[HALF:]))
            u = by_right(ie, tables, 6)
            v = by_right(io, tables, 7)
            s, d = u + v, u - v
            cr = lanes(s[:, :HALF], d[:, :HALF])
            ci = lanes(s[:, HALF:], d[:, HALF:])
            sr, si = patch[0], patch[1]
            wr, wi = waves[p, 0, m].astype(f32), waves[p, 1, m].astype(f32)
            gr, gi = wr * cr + wi * ci, wr * ci - wi * cr
            if m == 0:
                upd[p, 0], upd[p, 1] = gr, gi
            else:
                upd[p, 0], upd[p, 1] = upd[p, 0] + gr, upd[p, 1] + gi
            back[p, m, 0] = sr * cr + si * ci
            back[p, m, 1] = sr * ci - si * cr
        add_patch(p, 2, upd.at[p])

        @pl.when(p == 1)
        def _():
            halo_one.forward()

        return carry

    lax.fori_loop(0, POSITIONS, phase_one, 0)
    scale_two = send_rims(rim_two)
    halo_one.wait()
    widen(0)

    def phase_two(p, m):
        if m == 0:
            take_patch(p, upd.at[p])
        p0, p1 = halves(back[p, m, 0], back[p, m, 1])
        u = by_right(p0 + p1, tables, 8)
        v = by_right(p0 - p1, tables, 9)
        s, d = u + v, u - v
        re = lanes(s[:, :HALF], d[:, :HALF])
        im = lanes(s[:, HALF:], d[:, HALF:])
        u = by_left(rows(re[:HALF] + re[HALF:], im[:HALF] + im[HALF:]), tables, 10)
        v = by_left(rows(re[:HALF] - re[HALF:], im[:HALF] - im[HALF:]), tables, 11)
        s, d = u + v, u - v
        br = rows(s[:HALF], d[:HALF])
        bi = rows(s[HALF:], d[HALF:])
        pr, pi = probe[0, m], probe[1, m]
        ar, ai = upd[p, 0], upd[p, 1]
        gr, gi = pr * br + pi * bi, pr * bi - pi * br
        for part, value in enumerate((ar * br + ai * bi, ar * bi - ai * br)):
            for h in range(2):
                half = value[:, h * HALF : (h + 1) * HALF].reshape(16, 2, 8, HALF)
                gp[m, h, part] = gp[m, h, part] + half
        if m == 0:
            back[p, 0, 0], back[p, 0, 1] = gr, gi
        else:
            patch[0], patch[1] = back[p, 0, 0] + gr, back[p, 0, 1] + gi
            add_patch(p, 0, patch)

    def first_mode(p, carry):
        phase_two(p, 0)
        return carry

    def second_mode(p, carry):
        phase_two(p, 1)
        return carry

    def stage_one(m):
        return [send(gp.at[m, 1 - core], r1.at[m], pair_sems.at[0, m], other_core)]

    def stage_two(m):
        for l in range(2):
            s1[m, l] = gp[m, core, :, :, l] + r1[m, :, :, l]
        return [send(s1.at[m, 1 - layer], r2.at[m], pair_sems.at[1, m], other_layer)]

    def finish(copies):
        for copy in copies:
            copy.wait()

    lax.fori_loop(0, POSITIONS, first_mode, 0)
    one_a = stage_one(0)
    rim_two.forward()
    lax.fori_loop(0, 1, second_mode, 0)
    finish(one_a)
    two_a = stage_two(0)
    lax.fori_loop(1, POSITIONS, second_mode, 0)
    one_b = stage_one(1)
    scale_one = send_rims(rim_one)
    finish(two_a)
    finish(one_b)
    two_b = stage_two(1)
    rim_two.wait()
    finish(scale_two)
    rim_one.forward()
    acc = jnp.zeros((8, HALF), f32)

    def total_of(c, acc):
        for k in range(CHUNKS):
            part = pl.ds(k * 64, 64)
            total = grad[c, part, HALF : 2 * HALF]
            total = total + restored(in_codes.at[1, c], in_scales.at[1, c], k) * has_right
            total = total + restored(in_codes.at[0, c], in_scales.at[0, c], k) * has_left
            total_out[c, part] = total
            acc = acc + jnp.sum((total * total).reshape(8, 8, HALF), axis=0)
        return acc

    for c in (2, 3):
        acc = total_of(c, acc)
    finish(two_b)
    for m in range(2):
        for part in range(2):
            s2[part * 2 + m] = s1[m, layer, part] + r2[m, part]
    copies = []
    for j in range(1, 4):
        copies.append(send(s2.at[(x + j) % 4], r3.at[j - 1], sems3.at[j - 1], along_x(j)))
    finish(copies)
    s3[...] = s2[x] + r3[0] + r3[1] + r3[2]
    four = [send(s3.at[(zy + j) % 16], r4.at[j - 1], sems4.at[j - 1], along_zy(j)) for j in range(1, 16)]
    rim_one.wait()
    finish(scale_one)
    for c in (0, 1):
        acc = total_of(c, acc)
    finish(four)
    piece = s3[zy]
    for j in range(15):
        piece = piece + r4[j]
    fin[0] = piece
    gathers = [send(fin.at[0], fin.at[j], sems5.at[j - 1], along_group(j)) for j in range(1, 4)]
    object_row = jnp.sum(acc, axis=0, keepdims=True)
    probe_row = jnp.sum(piece * piece, axis=0, keepdims=True)
    top = lax.broadcasted_iota(jnp.int32, (8, HALF), 0) < 4
    q1[0] = jnp.where(top, object_row, probe_row)
    finish([send(q1.at[0], q1.at[j], sems6.at[j - 1], along_zy(j)) for j in range(1, 16)])
    both = q1[zy]
    for s in range(1, 16):
        both = both + q1[(zy + 16 - s) % 16]
    q2[0] = both
    finish([send(q2.at[0], q2.at[j], sems7.at[j - 1], along_spot(j)) for j in range(1, 16)])
    both = q2[spot]
    for s in range(1, 16):
        both = both + q2[(spot + 16 - s) % 16]
    squares_out[...] = both
    finish(gathers)
    for s in range(4):
        shard_out[s // 2 * 8 : s // 2 * 8 + 8, s % 2 * HALF : s % 2 * HALF + HALF] = fin[(g + 4 - s) % 4]


def final_kernel(own_obj, total, squares, shard, old_probe, object_new, probe_new):
    sums = jnp.sum(squares[...], axis=1, keepdims=True)
    object_step_size = object_step * lax.rsqrt(sums[0:1] * (1.0 / OBJECT_COUNT) + epsilon)
    probe_step_size = probe_step * lax.rsqrt(sums[4:5] * (1.0 / PROBE_COUNT) + epsilon)
    for c in range(4):
        object_new[c] = own_obj[c].astype(f32) - total[c] * object_step_size
    at = pl.multiple_of(lax.axis_index("tile") * 16, 16)
    probe_new[...] = old_probe[pl.ds(at, 16), :] - shard[...] * probe_step_size


def shards(object_slices, probe, mid_waves, amplitudes, row_offsets, col_offsets):
    tables = jnp.asarray(transform_tables())
    tile = (8, HALF)
    whole = (PX, PX)
    vmem = pl.BlockSpec(memory_space=pltpu.VMEM)
    smem = pl.BlockSpec(memory_space=pltpu.SMEM)
    anywhere = pl.BlockSpec(memory_space=pl.ANY)
    sem = pltpu.SemaphoreType.DMA
    strip = jax.ShapeDtypeStruct(object_slices.shape, f32)
    shard = jax.ShapeDtypeStruct((16, PX), f32)
    total, squares, shard_sum = pl.pallas_call(
        kernel,
        out_shape=[strip, jax.ShapeDtypeStruct(tile, f32), shard],
        in_specs=[smem, smem, vmem] + [anywhere] * 4,
        out_specs=[vmem] * 3,
        scratch_shapes=[
            pltpu.VMEM((2, 2, *whole), f32),
            pltpu.VMEM((3, 2, 2, *whole), bf16),
            pltpu.VMEM((3, *whole), bf16),
            pltpu.VMEM(tables.shape, bf16),
            pltpu.VMEM((2, 4, ROWS, HALF), bf16),
            pltpu.VMEM((2, ROWS + 8, 3 * HALF), f32),
            pltpu.VMEM((4, ROWS, 3 * HALF), f32),
            pltpu.VMEM((2, ROWS + PX, 3 * HALF), f32),
            pltpu.VMEM((2, *whole), f32),
            pltpu.VMEM((2, 2, *whole), f32),
            pltpu.VMEM((3, 2, 2, *whole), f32),
            pltpu.VMEM((3, 2, *whole), f32),
            pltpu.VMEM((3, *whole), f32),
            pltpu.VMEM((2, 2, 2, 16, 2, *tile), f32),
            pltpu.VMEM((2, 4, ROWS, HALF), jnp.int16),
            pltpu.VMEM((2, 4, *tile), f32),
            pltpu.VMEM((2, 4, ROWS, HALF), jnp.int16),
            pltpu.VMEM((2, 4, *tile), f32),
            pltpu.VMEM((2, 2, ROWS, HALF), bf16),
            pltpu.VMEM((2, 2, ROWS, HALF), jnp.int16),
            pltpu.VMEM((2, 2, 16, 2, *tile), f32),
            pltpu.VMEM((2, 2, 2, 16, *tile), f32),
            pltpu.VMEM((2, 2, 16, *tile), f32),
            pltpu.VMEM((4, 16, *tile), f32),
            pltpu.VMEM((3, 16, *tile), f32),
            pltpu.VMEM((16, *tile), f32),
            pltpu.VMEM((15, *tile), f32),
            pltpu.VMEM((4, *tile), f32),
            pltpu.VMEM((16, *tile), f32),
            pltpu.VMEM((16, *tile), f32),
            sem((4,)), sem((4, 2, 2)), sem((4, 2, PIECES, 2)), sem((4, 2, PIECES, 2)), sem((4, 2, PIECES)),
            sem((2, 2, 2)), sem((2, 2, 2)),
            sem((3, 2)), sem((15, 2)), sem((3, 2)), sem((15, 2)), sem((15, 2)),
        ],
        compiler_params=pltpu.CompilerParams(
            collective_id=0, has_side_effects=True, vmem_limit_bytes=56 * 1024 * 1024
        ),
        name="update",
    )(
        row_offsets[0, 0], col_offsets[0, 0], object_slices, probe.reshape(2, 2, *whole),
        mid_waves[0, 0], amplitudes[0, 0], tables,
    )
    return pl.pallas_call(
        final_kernel,
        out_shape=[strip, shard],
        in_specs=[vmem] * 5,
        out_specs=[vmem] * 2,
        compiler_params=pltpu.CompilerParams(vmem_limit_bytes=16 * 1024 * 1024),
        name="final",
    )(object_slices, total, squares, shard_sum, probe)


def solution(mesh):
    return jax.shard_map(
        shards,
        mesh=mesh,
        in_specs=(
            P(None, "group", "tile"),
            P(),
            P("group", "tile", None, None, None, None, None),
            P("group", "tile", None, None, None),
            P("group", "tile", None),
            P("group", "tile", None),
        ),
        out_specs=(P(None, "group", "tile"), P("tile", None)),
        check_vma=False,
    )
```

```python
import numpy as np
import ml_dtypes
import jax
import jax.numpy as jnp
from jax import lax
from jax.sharding import PartitionSpec as P
from jax.experimental import pallas as pl
from jax.experimental.pallas import tpu as pltpu

phase_rate = 0.25
floor_level = 0.5
object_step = 0.5
probe_step = 0.5
epsilon = 1e-06
f32 = jnp.float32
bf16 = jnp.bfloat16
PX = 256
HALF = 128
TALL = PX + 8
ROWS = 512
POSITIONS = 3
CHUNKS = 8
PIECES = 4
STEP = 32
CHUNK_ROWS = ROWS // PIECES
LEVELS = 32767.0
LEVELS_TWO = 32000.0
OBJECT_COUNT = 4 * 2048 * 8192
PROBE_COUNT = 4 * PX * PX


def right_form(m):
    return np.block([[m.real, m.imag], [-m.imag, m.real]])


def left_form(m):
    return np.block([[m.real, -m.imag], [m.imag, m.real]])


def transform_tables():
    n = np.arange(HALF)[:, None]
    k = np.arange(HALF)[None, :]
    root = -2j * np.pi / PX
    even = np.exp(root * ((2 * n * k) % PX)) / np.sqrt(PX)
    odd = np.exp(root * ((n * (2 * k + 1)) % PX)) / np.sqrt(PX)
    freq = np.arange(PX)
    freq = np.where(freq < HALF, freq, freq - PX)
    phase = np.exp(2j * np.pi * phase_rate * freq * freq / PX)
    ring = np.fft.ifft(phase)
    i, j = np.meshgrid(np.arange(HALF), np.arange(HALF), indexing="ij")
    near, far = ring[(i - j) % PX], ring[(i - j + HALF) % PX]
    plus, minus = (near + far) / 2, (near - far) / 2
    forms = [
        right_form(even), right_form(odd),
        left_form(even.T), left_form(odd.T),
        left_form(even.conj()), left_form(odd.conj()),
        right_form(even.conj().T), right_form(odd.conj().T),
        right_form(plus.T), right_form(minus.T),
        left_form(plus), left_form(minus),
    ]
    whole = np.stack(forms)
    high = whole.astype(ml_dtypes.bfloat16)
    low = (whole - high.astype(np.float64)).astype(ml_dtypes.bfloat16)
    return np.stack([high, low], axis=1)


def split(x):
    high = x.astype(bf16)
    return high, (x - high.astype(f32)).astype(bf16)


def by_right(high, low, tables, index):
    h, t = high[...], tables[index, 0]
    return jnp.dot(
        jnp.concatenate([h, low[...], h], axis=1),
        jnp.concatenate([t, t, tables[index, 1]], axis=0),
        preferred_element_type=f32,
    )


def by_left(high, low, tables, index):
    h, t = high[...], tables[index, 0]
    return jnp.dot(
        jnp.concatenate([t, t, tables[index, 1]], axis=1),
        jnp.concatenate([h, low[...], h], axis=0),
        preferred_element_type=f32,
    )


def put(high, low, at, value):
    high[at : at + STEP], low[at : at + STEP] = split(value)


def lanes(a, b):
    return jnp.concatenate([a, b], axis=1)


def rows(a, b):
    return jnp.concatenate([a, b], axis=0)


def halves(re, im):
    return lanes(re[:, :HALF], im[:, :HALF]), lanes(re[:, HALF:], im[:, HALF:])


def quantised(values, codes, scales):
    for k in range(CHUNKS):
        part = values[k * 64 : (k + 1) * 64]
        top = jnp.maximum(jnp.max(jnp.abs(part), axis=0, keepdims=True), 1e-30)
        scales[k : k + 1] = top * (1.0 / LEVELS)
        codes[k * 64 : (k + 1) * 64] = jnp.round(part * (LEVELS / top)).astype(jnp.int32).astype(jnp.int16)


def restored(codes, scales, k):
    return codes[k * 64 : (k + 1) * 64].astype(jnp.int32).astype(f32) * scales[k : k + 1]


def kernel(row_ref, col_ref, own_obj, probe_hbm, waves_hbm, amps_hbm, tables_hbm,
           total_out, squares_out, shard_out,
           probe, waves, amps, tables, halo, obj, grad, pad, patch, far, back_high, back_low, highs, lows, products, upd, sorted_amps, gp,
           out_codes, out_scales, in_codes, in_scales,
           halo_relay, code_relay, probe_codes, r1, s3, r4, fin, q1, q2,
           load_sems, direct_sems, chunk_sems, relay_sems, onward_sems, scale_sems,
           sems3, sems4, sems5, sems6, sems7):
    g = lax.axis_index("group")
    t = lax.axis_index("tile")
    x, zy = t // 16, t % 16
    spot = x * 4 + g
    right = (g, (t + 1) % 64)
    left = (g, (t + 63) % 64)
    y = zy % 4
    onward = ((g, (t + 4) % 64), (g, (t + 60) % 64))
    wrapped = ((g, t - y), (g, t - y + 3))
    at_end = (y == 3, y == 0)
    at_start = (y == 0, y == 3)
    def along_zy(j):
        return (g, x * 16 + (zy + j) % 16)

    def along_group(j):
        return ((g + j) % 4, t)

    def along_spot(j):
        to = (spot + j) % 16
        return (to % 4, to // 4 * 16 + zy)

    loads = [
        pltpu.make_async_copy(src, dst, load_sems.at[i])
        for i, (src, dst) in enumerate(
            [(amps_hbm, amps), (waves_hbm, waves), (tables_hbm, tables), (probe_hbm, probe)]
        )
    ]
    for load in loads:
        load.start()
    barrier = pltpu.get_barrier_semaphore()
    partners = [right, left, *onward] + [along_zy(j) for j in range(1, 16)] + [along_spot(j) for j in range(1, 16)]
    for partner in partners:
        pl.semaphore_signal(barrier, inc=1, device_id=partner, device_id_type=pl.DeviceIdType.MESH)
    pl.semaphore_wait(barrier, len(partners))

    def send(src, dst, sems, device):
        copy = pltpu.make_async_remote_copy(
            src_ref=src, dst_ref=dst, send_sem=sems.at[0], recv_sem=sems.at[1],
            device_id=device, device_id_type=pl.DeviceIdType.MESH,
        )
        copy.start()
        return copy

    class Swap:
        def __init__(self, number, src, dst, relay, first):
            self.number, self.src, self.dst, self.relay, self.first = number, src, dst, relay, first

        def near(self, side):
            return right if side == 0 else left

        def chunk(self, ref, k):
            return ref.at[pl.ds(k * CHUNK_ROWS, CHUNK_ROWS)]

        def copy(self, src, dst, send_sem, recv_sem, device):
            return pltpu.make_async_remote_copy(
                src_ref=src, dst_ref=dst, send_sem=send_sem, recv_sem=recv_sem,
                device_id=device, device_id_type=pl.DeviceIdType.MESH,
            )

        def direct(self, side):
            sems = direct_sems.at[self.number, side]
            return self.copy(
                self.src(side).at[self.first], self.dst(side).at[self.first], sems.at[0], sems.at[1], self.near(side)
            )

        def plain(self, side, k):
            sems = chunk_sems.at[self.number, side, k]
            second = self.first + 1
            return self.copy(
                self.chunk(self.src(side).at[second], k), self.chunk(self.dst(side).at[second], k),
                sems.at[0], sems.at[1], self.near(side),
            )

        def detour(self, side, k):
            sems = relay_sems.at[self.number, side, k]
            return self.copy(
                self.chunk(self.src(side).at[self.first + 1], k), self.chunk(self.relay(side), k),
                sems.at[0], sems.at[1], wrapped[side],
            )

        def forwarded(self, side, k):
            return self.copy(
                self.chunk(self.relay(side), k), self.chunk(self.dst(side).at[self.first + 1], k),
                onward_sems.at[self.number, side, k], chunk_sems.at[self.number, side, k].at[1], onward[side],
            )

        def start(self):
            for side in range(2):
                @pl.when(at_end[side])
                def _():
                    for k in range(PIECES):
                        self.detour(side, k).start()

                @pl.when(jnp.logical_not(at_end[side]))
                def _():
                    for k in range(PIECES):
                        self.plain(side, k).start()

            for side in range(2):
                self.direct(side).start()

        def forward(self):
            for side in range(2):
                @pl.when(at_start[side])
                def _():
                    for k in range(PIECES):
                        self.detour(side, k).wait_recv()
                        self.forwarded(side, k).start()

        def wait(self):
            for side in range(2):
                for k in range(PIECES):
                    self.plain(side, k).wait_recv()
                self.direct(side).wait()

                @pl.when(at_end[side])
                def _():
                    for k in range(PIECES):
                        self.detour(side, k).wait_send()

                @pl.when(jnp.logical_not(at_end[side]))
                def _():
                    for k in range(PIECES):
                        self.plain(side, k).wait_send()

                @pl.when(at_start[side])
                def _():
                    for k in range(PIECES):
                        self.forwarded(side, k).wait_send()

    def halo_swap(number, first):
        return Swap(number, lambda side: own_obj, lambda side: halo.at[side], lambda side: halo_relay.at[number, side], first)

    def rim_swap(number, first):
        return Swap(
            number, lambda side: out_codes.at[side], lambda side: in_codes.at[side],
            lambda side: code_relay.at[number - 2, side], first,
        )

    halo_two, halo_one = halo_swap(0, 2), halo_swap(1, 0)
    rim_two, rim_one = rim_swap(2, 2), rim_swap(3, 0)
    halo_two.start()

    at_row = lax.broadcasted_iota(jnp.int32, (PX, PX), 0)
    at_col = lax.broadcasted_iota(jnp.int32, (PX, PX), 1)
    sort_row = (at_col == jnp.where(at_row < HALF, 2 * at_row, 2 * at_row - PX + 1)).astype(f32).astype(bf16)
    sort_col = (at_row == jnp.where(at_col < HALF, 2 * at_col, 2 * at_col - PX + 1)).astype(f32).astype(bf16)
    grad[...] = jnp.zeros_like(grad)
    pad[:, :PX] = jnp.zeros((2, PX, 3 * HALF), f32)
    pad[:, PX + TALL :] = jnp.zeros((2, PX - 8, 3 * HALF), f32)
    obj[:, ROWS:, :] = jnp.zeros((2, 8, 3 * HALF), f32)
    gp[...] = jnp.zeros_like(gp)
    loads[0].wait()

    def sort_amps(p, carry):
        amp = jnp.dot(sort_row, amps[p], preferred_element_type=f32).astype(bf16)
        sorted_amps[p] = jnp.dot(amp, sort_col, preferred_element_type=f32)
        return carry

    lax.fori_loop(0, POSITIONS, sort_amps, 0)
    has_left = jnp.where(t > 0, 1.0, 0.0)
    has_right = jnp.where(t < 63, 1.0, 0.0)

    def widen(first):
        for c in range(2):
            obj[c, :ROWS, :HALF] = halo[0, first + c].astype(f32) * has_left
            obj[c, :ROWS, HALF : 2 * HALF] = own_obj[first + c].astype(f32)
            obj[c, :ROWS, 2 * HALF :] = halo[1, first + c].astype(f32) * has_right

    def offsets(p):
        row_at = row_ref[p]
        return lax.div(row_at, 8), lax.rem(row_at, 8), col_ref[p]

    def take_patch(p, dst):
        row_tile, row_rest, col_at = offsets(p)
        pick = (
            lax.broadcasted_iota(jnp.int32, (3 * HALF, PX), 0)
            == lax.broadcasted_iota(jnp.int32, (3 * HALF, PX), 1) + col_at
        ).astype(f32).astype(bf16)
        for c in range(2):
            raw = obj[c, pl.ds(row_tile * 8, TALL), :].astype(bf16)
            wide = jnp.dot(raw, pick, preferred_element_type=f32)
            dst[c] = pltpu.roll(wide, TALL - row_rest, 0)[:PX]

    def add_patch(p, first, values):
        row_tile, row_rest, col_at = offsets(p)
        place = (
            lax.broadcasted_iota(jnp.int32, (PX, 3 * HALF), 1)
            == lax.broadcasted_iota(jnp.int32, (PX, 3 * HALF), 0) + col_at
        ).astype(f32).astype(bf16)
        for c in range(2):
            high, low = split(values[c])
            moved = jnp.dot(lanes(high, low), rows(place, place), preferred_element_type=f32)
            moved = rows(moved, jnp.zeros((TALL - PX, 3 * HALF), f32))
            pad[c, PX : PX + TALL] = pltpu.roll(moved, row_rest, 0)
            grad[first + c] = grad[first + c] + pad[c, pl.ds((PX // 8 - row_tile) * 8, ROWS), :]

    def send_rims(swap):
        first = swap.first
        copies = []
        for side in range(2):
            from_lane = 2 * HALF * (1 - side)
            for c in range(2):
                quantised(
                    grad[first + c, :, from_lane : from_lane + HALF],
                    out_codes.at[side, first + c], out_scales.at[side, first + c],
                )
        swap.start()
        for side in range(2):
            part = pl.ds(first, 2)
            copies.append(
                send(out_scales.at[side, part], in_scales.at[side, part], scale_sems.at[side, first // 2], swap.near(side))
            )
        return copies

    for load in loads[1:]:
        load.wait()
    halo_two.forward()
    halo_two.wait()
    halo_one.start()
    widen(2)

    def stacked_halves(high, low, product, mixed):
        for r in range(0, HALF, STEP):
            for i in range(2):
                here = pl.ds(r, STEP), slice(i * HALF, i * HALF + HALF)
                there = pl.ds(HALF + r, STEP), slice(i * HALF, i * HALF + HALF)
                u, v = product[0, here[0], here[1]], product[1, here[0], here[1]]
                top = lanes(u + v, u - v) if mixed else lanes(u, v)
                u, v = product[0, there[0], there[1]], product[1, there[0], there[1]]
                bottom = lanes(u + v, u - v) if mixed else lanes(u, v)
                put(high.at[0], low.at[0], i * HALF + r, top + bottom)
                put(high.at[1], low.at[1], i * HALF + r, top - bottom)

    def phase_one(p, carry):
        take_patch(p, patch)
        for m in range(2):
            high, low, product = highs.at[m], lows.at[m], products.at[m]
            for r in range(0, PX, STEP):
                part = pl.ds(r, STEP)
                sr, si = patch[0, part], patch[1, part]
                wr, wi = waves[p, 0, m, part].astype(f32), waves[p, 1, m, part].astype(f32)
                p0, p1 = halves(wr * sr - wi * si, wr * si + wi * sr)
                put(high.at[0], low.at[0], r, p0 + p1)
                put(high.at[1], low.at[1], r, p0 - p1)
            for e in range(2):
                product[e] = by_right(high.at[e], low.at[e], tables, e)
            stacked_halves(high, low, product, False)
            for e in range(2):
                far[m, e] = by_left(high.at[e], low.at[e], tables, 2 + e)
        for e in range(2):
            for r in range(0, HALF, STEP):
                real, imag = pl.ds(r, STEP), pl.ds(HALF + r, STEP)
                zs = [(far[m, e, real], far[m, e, imag]) for m in range(2)]
                power = 0.0
                for zr, zi in zs:
                    power = power + (zr * zr + zi * zi)
                amp = sorted_amps[p, e * HALF + r : e * HALF + r + STEP]
                factor = 1.0 - amp * jnp.minimum(lax.rsqrt(power), 1.0 / floor_level)
                for m, (zr, zi) in enumerate(zs):
                    put(highs.at[m, e], lows.at[m, e], r, zr * factor)
                    put(highs.at[m, e], lows.at[m, e], HALF + r, zi * factor)
        for m in range(2):
            high, low, product = highs.at[m], lows.at[m], products.at[m]
            for e in range(2):
                product[e] = by_left(high.at[e], low.at[e], tables, 4 + e)
            for r in range(0, HALF, STEP):
                real, imag = pl.ds(r, STEP), pl.ds(HALF + r, STEP)
                ur, ui, vr, vi = product[0, real], product[0, imag], product[1, real], product[1, imag]
                for at, re, im in ((r, ur + vr, ui + vi), (HALF + r, ur - vr, ui - vi)):
                    even, odd = halves(re, im)
                    put(high.at[0], low.at[0], at, even)
                    put(high.at[1], low.at[1], at, odd)
            for e in range(2):
                product[e] = by_right(high.at[e], low.at[e], tables, 6 + e)
            for r in range(0, PX, STEP):
                part = pl.ds(r, STEP)
                u, v = product[0, part], product[1, part]
                s, d = u + v, u - v
                cr = lanes(s[:, :HALF], d[:, :HALF])
                ci = lanes(s[:, HALF:], d[:, HALF:])
                sr, si = patch[0, part], patch[1, part]
                wr, wi = waves[p, 0, m, part].astype(f32), waves[p, 1, m, part].astype(f32)
                gr, gi = wr * cr + wi * ci, wr * ci - wi * cr
                if m == 0:
                    upd[p, 0, part], upd[p, 1, part] = gr, gi
                else:
                    upd[p, 0, part], upd[p, 1, part] = upd[p, 0, part] + gr, upd[p, 1, part] + gi
                p0, p1 = halves(sr * cr + si * ci, sr * ci - si * cr)
                put(back_high.at[p, m, 0], back_low.at[p, m, 0], r, p0 + p1)
                put(back_high.at[p, m, 1], back_low.at[p, m, 1], r, p0 - p1)
        add_patch(p, 2, upd.at[p])

        @pl.when(p == 1)
        def _():
            halo_one.forward()

        return carry

    lax.fori_loop(0, POSITIONS, phase_one, 0)
    scale_two = send_rims(rim_two)
    halo_one.wait()
    widen(0)

    def phase_two(p, carry):
        take_patch(p, patch)
        for m in range(2):
            high, low, product = highs.at[m], lows.at[m], products.at[m]
            for e in range(2):
                product[e] = by_right(back_high.at[p, m, e], back_low.at[p, m, e], tables, 8 + e)
            stacked_halves(high, low, product, True)
            for e in range(2):
                far[m, e] = by_left(high.at[e], low.at[e], tables, 10 + e)
        for r in range(0, HALF, STEP):
            real, imag = pl.ds(r, STEP), pl.ds(HALF + r, STEP)
            for bottom in range(2):
                part = pl.ds(bottom * HALF + r, STEP)
                ar, ai = patch[0, part], patch[1, part]
                sum_r, sum_i = 0.0, 0.0
                for m in range(2):
                    ur, ui, vr, vi = far[m, 0, real], far[m, 0, imag], far[m, 1, real], far[m, 1, imag]
                    br, bi = (ur - vr, ui - vi) if bottom else (ur + vr, ui + vi)
                    pr, pi = probe[0, m, part], probe[1, m, part]
                    sum_r = sum_r + (pr * br + pi * bi)
                    sum_i = sum_i + (pr * bi - pi * br)
                    tile_at = (bottom * HALF + r) // 16
                    for c, value in enumerate((ar * br + ai * bi, ar * bi - ai * br)):
                        for h in range(2):
                            half = value[:, h * HALF : (h + 1) * HALF].reshape(STEP // 16, 2, 8, HALF)
                            for l in range(2):
                                to = c * 2 + m, l * 2 + h, pl.ds(tile_at, STEP // 16)
                                gp[to] = gp[to] + half[:, l]
                upd[p, 0, part], upd[p, 1, part] = sum_r, sum_i
        return carry

    def scatter_one(p, carry):
        add_patch(p, 0, upd.at[p])
        return carry

    def finish(copies):
        for copy in copies:
            copy.wait()

    def code_piece(q, carry):
        values = gp[q // 4, q % 4].reshape(HALF, HALF)
        largest = jnp.maximum(jnp.max(jnp.abs(values), axis=0, keepdims=True), 1e-30)
        power = jnp.ceil(jnp.log2(largest))
        scaled = values * (LEVELS_TWO * jnp.exp2(-power))
        probe_codes[q, :HALF] = jnp.round(scaled).astype(jnp.int32).astype(jnp.int16)
        probe_codes[q, HALF:] = jnp.broadcast_to(power, (16, HALF)).astype(jnp.int32).astype(jnp.int16)
        return carry

    lax.fori_loop(0, 1, phase_two, 0)
    rim_two.forward()
    lax.fori_loop(1, POSITIONS, phase_two, 0)
    lax.fori_loop(0, 16, code_piece, 0)
    one = [
        send(probe_codes.at[(spot + j) % 16], r1.at[j - 1], sems3.at[j - 1], along_spot(j)) for j in range(1, 16)
    ]
    lax.fori_loop(0, POSITIONS, scatter_one, 0)
    scale_one = send_rims(rim_one)
    rim_two.wait()
    finish(scale_two)
    rim_one.forward()
    acc = jnp.zeros((8, HALF), f32)

    def total_of(c, acc):
        for k in range(CHUNKS):
            part = pl.ds(k * 64, 64)
            total = grad[c, part, HALF : 2 * HALF]
            total = total + restored(in_codes.at[1, c], in_scales.at[1, c], k) * has_right
            total = total + restored(in_codes.at[0, c], in_scales.at[0, c], k) * has_left
            total_out[c, part] = total
            acc = acc + jnp.sum((total * total).reshape(8, 8, HALF), axis=0)
        return acc

    for c in (2, 3):
        acc = total_of(c, acc)
    finish(one)
    mine = gp[x, g]
    for j in range(15):
        power = r1[j, HALF:].astype(jnp.int32).astype(f32)[:1]
        codes = r1[j, :HALF].astype(jnp.int32).astype(f32)
        mine = mine + (codes * (jnp.exp2(power) * (1.0 / LEVELS_TWO))).reshape(16, 8, HALF)
    s3[...] = mine
    four = [send(s3.at[(zy + j) % 16], r4.at[j - 1], sems4.at[j - 1], along_zy(j)) for j in range(1, 16)]
    rim_one.wait()
    finish(scale_one)
    for c in (0, 1):
        acc = total_of(c, acc)
    finish(four)
    piece = s3[zy]
    for j in range(15):
        piece = piece + r4[j]
    fin[0] = piece
    gathers = [send(fin.at[0], fin.at[j], sems5.at[j - 1], along_group(j)) for j in range(1, 4)]
    object_row = jnp.sum(acc, axis=0, keepdims=True)
    probe_row = jnp.sum(piece * piece, axis=0, keepdims=True)
    top = lax.broadcasted_iota(jnp.int32, (8, HALF), 0) < 4
    q1[0] = jnp.where(top, object_row, probe_row)
    finish([send(q1.at[0], q1.at[j], sems6.at[j - 1], along_zy(j)) for j in range(1, 16)])
    both = q1[zy]
    for s in range(1, 16):
        both = both + q1[(zy + 16 - s) % 16]
    q2[0] = both
    finish([send(q2.at[0], q2.at[j], sems7.at[j - 1], along_spot(j)) for j in range(1, 16)])
    both = q2[spot]
    for s in range(1, 16):
        both = both + q2[(spot + 16 - s) % 16]
    squares_out[...] = both
    finish(gathers)
    for s in range(4):
        shard_out[s // 2 * 8 : s // 2 * 8 + 8, s % 2 * HALF : s % 2 * HALF + HALF] = fin[(g + 4 - s) % 4]


def final_kernel(own_obj, total, squares, shard, old_probe, object_new, probe_new):
    sums = jnp.sum(squares[...], axis=1, keepdims=True)
    object_step_size = object_step * lax.rsqrt(sums[0:1] * (1.0 / OBJECT_COUNT) + epsilon)
    probe_step_size = probe_step * lax.rsqrt(sums[4:5] * (1.0 / PROBE_COUNT) + epsilon)
    for c in range(4):
        object_new[c] = own_obj[c].astype(f32) - total[c] * object_step_size
    at = pl.multiple_of(lax.axis_index("tile") * 16, 16)
    probe_new[...] = old_probe[pl.ds(at, 16), :] - shard[...] * probe_step_size


def shards(object_slices, probe, mid_waves, amplitudes, row_offsets, col_offsets):
    tables = jnp.asarray(transform_tables())
    tile = (8, HALF)
    whole = (PX, PX)
    vmem = pl.BlockSpec(memory_space=pltpu.VMEM)
    smem = pl.BlockSpec(memory_space=pltpu.SMEM)
    anywhere = pl.BlockSpec(memory_space=pl.ANY)
    sem = pltpu.SemaphoreType.DMA
    strip = jax.ShapeDtypeStruct(object_slices.shape, f32)
    shard = jax.ShapeDtypeStruct((16, PX), f32)
    total, squares, shard_sum = pl.pallas_call(
        kernel,
        out_shape=[strip, jax.ShapeDtypeStruct(tile, f32), shard],
        in_specs=[smem, smem, vmem] + [anywhere] * 4,
        out_specs=[vmem] * 3,
        scratch_shapes=[
            pltpu.VMEM((2, 2, *whole), f32),
            pltpu.VMEM((3, 2, 2, *whole), bf16),
            pltpu.VMEM((3, *whole), bf16),
            pltpu.VMEM(tables.shape, bf16),
            pltpu.VMEM((2, 4, ROWS, HALF), bf16),
            pltpu.VMEM((2, ROWS + 8, 3 * HALF), f32),
            pltpu.VMEM((4, ROWS, 3 * HALF), f32),
            pltpu.VMEM((2, ROWS + PX, 3 * HALF), f32),
            pltpu.VMEM((2, *whole), f32),
            pltpu.VMEM((2, 2, *whole), f32),
            pltpu.VMEM((3, 2, 2, *whole), bf16),
            pltpu.VMEM((3, 2, 2, *whole), bf16),
            pltpu.VMEM((2, 2, *whole), bf16),
            pltpu.VMEM((2, 2, *whole), bf16),
            pltpu.VMEM((2, 2, *whole), f32),
            pltpu.VMEM((3, 2, *whole), f32),
            pltpu.VMEM((3, *whole), f32),
            pltpu.VMEM((4, 4, 16, *tile), f32),
            pltpu.VMEM((2, 4, ROWS, HALF), jnp.int16),
            pltpu.VMEM((2, 4, *tile), f32),
            pltpu.VMEM((2, 4, ROWS, HALF), jnp.int16),
            pltpu.VMEM((2, 4, *tile), f32),
            pltpu.VMEM((2, 2, ROWS, HALF), bf16),
            pltpu.VMEM((2, 2, ROWS, HALF), jnp.int16),
            pltpu.VMEM((16, HALF + 16, HALF), jnp.int16),
            pltpu.VMEM((15, HALF + 16, HALF), jnp.int16),
            pltpu.VMEM((16, *tile), f32),
            pltpu.VMEM((15, *tile), f32),
            pltpu.VMEM((4, *tile), f32),
            pltpu.VMEM((16, *tile), f32),
            pltpu.VMEM((16, *tile), f32),
            sem((4,)), sem((4, 2, 2)), sem((4, 2, PIECES, 2)), sem((4, 2, PIECES, 2)), sem((4, 2, PIECES)),
            sem((2, 2, 2)),
            sem((15, 2)), sem((15, 2)), sem((3, 2)), sem((15, 2)), sem((15, 2)),
        ],
        compiler_params=pltpu.CompilerParams(
            collective_id=0, has_side_effects=True, vmem_limit_bytes=56 * 1024 * 1024
        ),
        name="update",
    )(
        row_offsets[0, 0], col_offsets[0, 0], object_slices, probe.reshape(2, 2, *whole),
        mid_waves[0, 0], amplitudes[0, 0], tables,
    )
    return pl.pallas_call(
        final_kernel,
        out_shape=[strip, shard],
        in_specs=[vmem] * 5,
        out_specs=[vmem] * 2,
        compiler_params=pltpu.CompilerParams(vmem_limit_bytes=16 * 1024 * 1024),
        name="final",
    )(object_slices, total, squares, shard_sum, probe)


def solution(mesh):
    return jax.shard_map(
        shards,
        mesh=mesh,
        in_specs=(
            P(None, "group", "tile"),
            P(),
            P("group", "tile", None, None, None, None, None),
            P("group", "tile", None, None, None),
            P("group", "tile", None),
            P("group", "tile", None),
        ),
        out_specs=(P(None, "group", "tile"), P("tile", None)),
        check_vma=False,
    )
```

```python
import numpy as np
import ml_dtypes
import jax
import jax.numpy as jnp
from jax import lax
from jax.sharding import PartitionSpec as P
from jax.experimental import pallas as pl
from jax.experimental.pallas import tpu as pltpu

phase_rate = 0.25
floor_level = 0.5
object_step = 0.5
probe_step = 0.5
epsilon = 1e-06
f32 = jnp.float32
bf16 = jnp.bfloat16
PX = 256
HALF = 128
TALL = PX + 8
ROWS = 512
POSITIONS = 3
CHUNKS = 8
PIECES = 2
STEP = 32
CHUNK_ROWS = ROWS // PIECES
LEVELS = 32767.0
LEVELS_TWO = 32000.0
OBJECT_COUNT = 4 * 2048 * 8192
PROBE_COUNT = 4 * PX * PX


def right_form(m):
    return np.block([[m.real, m.imag], [-m.imag, m.real]])


def left_form(m):
    return np.block([[m.real, -m.imag], [m.imag, m.real]])


def transform_tables():
    n = np.arange(HALF)[:, None]
    k = np.arange(HALF)[None, :]
    root = -2j * np.pi / PX
    even = np.exp(root * ((2 * n * k) % PX)) / np.sqrt(PX)
    odd = np.exp(root * ((n * (2 * k + 1)) % PX)) / np.sqrt(PX)
    freq = np.arange(PX)
    freq = np.where(freq < HALF, freq, freq - PX)
    phase = np.exp(2j * np.pi * phase_rate * freq * freq / PX)
    ring = np.fft.ifft(phase)
    i, j = np.meshgrid(np.arange(HALF), np.arange(HALF), indexing="ij")
    near, far = ring[(i - j) % PX], ring[(i - j + HALF) % PX]
    plus, minus = (near + far) / 2, (near - far) / 2
    forms = [
        right_form(even), right_form(odd),
        left_form(even.T), left_form(odd.T),
        left_form(even.conj()), left_form(odd.conj()),
        right_form(even.conj().T), right_form(odd.conj().T),
        right_form(plus.T), right_form(minus.T),
        left_form(plus), left_form(minus),
    ]
    whole = np.stack(forms)
    high = whole.astype(ml_dtypes.bfloat16)
    low = (whole - high.astype(np.float64)).astype(ml_dtypes.bfloat16)
    return np.stack([high, low], axis=1)


def split(x):
    high = x.astype(bf16)
    return high, (x - high.astype(f32)).astype(bf16)


def by_right(high, low, tables, index):
    h, t = high[...], tables[index, 0]
    return jnp.dot(
        jnp.concatenate([h, low[...], h], axis=1),
        jnp.concatenate([t, t, tables[index, 1]], axis=0),
        preferred_element_type=f32,
    )


def by_left(high, low, tables, index):
    h, t = high[...], tables[index, 0]
    return jnp.dot(
        jnp.concatenate([t, t, tables[index, 1]], axis=1),
        jnp.concatenate([h, low[...], h], axis=0),
        preferred_element_type=f32,
    )


def put(high, low, at, value):
    high[at : at + STEP], low[at : at + STEP] = split(value)


def lanes(a, b):
    return jnp.concatenate([a, b], axis=1)


def rows(a, b):
    return jnp.concatenate([a, b], axis=0)


def halves(re, im):
    return lanes(re[:, :HALF], im[:, :HALF]), lanes(re[:, HALF:], im[:, HALF:])


def quantised(values, codes, scales):
    for k in range(CHUNKS):
        part = values[k * 64 : (k + 1) * 64]
        top = jnp.maximum(jnp.max(jnp.abs(part), axis=0, keepdims=True), 1e-30)
        scales[k : k + 1] = top * (1.0 / LEVELS)
        codes[k * 64 : (k + 1) * 64] = jnp.round(part * (LEVELS / top)).astype(jnp.int32).astype(jnp.int16)


def restored(codes, scales, k):
    return codes[k * 64 : (k + 1) * 64].astype(jnp.int32).astype(f32) * scales[k : k + 1]


def kernel(row_ref, col_ref, own_obj, probe_hbm, waves_hbm, amps_hbm, tables_hbm,
           total_out, squares_out, shard_out,
           probe, waves, amps, tables, halo, obj, grad, pad, patch, far, back_high, back_low, highs, lows, products, upd, sorted_amps, gp,
           out_codes, out_scales, in_codes, in_scales,
           halo_relay, code_relay, probe_codes, r1, s3, r4, fin, q1, q2,
           load_sems, direct_sems, chunk_sems, relay_sems, onward_sems, scale_sems,
           sems3, sems4, sems5, sems6, sems7):
    g = lax.axis_index("group")
    t = lax.axis_index("tile")
    x, zy = t // 16, t % 16
    spot = x * 4 + g
    right = (g, (t + 1) % 64)
    left = (g, (t + 63) % 64)
    y = zy % 4
    onward = ((g, (t + 4) % 64), (g, (t + 60) % 64))
    wrapped = ((g, t - y), (g, t - y + 3))
    at_end = (y == 3, y == 0)
    at_start = (y == 0, y == 3)
    def along_zy(j):
        return (g, x * 16 + (zy + j) % 16)

    def along_group(j):
        return ((g + j) % 4, t)

    def along_spot(j):
        to = (spot + j) % 16
        return (to % 4, to // 4 * 16 + zy)

    loads = [
        pltpu.make_async_copy(src, dst, load_sems.at[i])
        for i, (src, dst) in enumerate(
            [(amps_hbm, amps), (waves_hbm, waves), (tables_hbm, tables), (probe_hbm, probe)]
        )
    ]
    for load in loads:
        load.start()
    barrier = pltpu.get_barrier_semaphore()
    partners = [right, left, *onward] + [along_zy(j) for j in range(1, 16)] + [along_spot(j) for j in range(1, 16)]
    for partner in partners:
        pl.semaphore_signal(barrier, inc=1, device_id=partner, device_id_type=pl.DeviceIdType.MESH)
    pl.semaphore_wait(barrier, len(partners))

    def send(src, dst, sems, device):
        copy = pltpu.make_async_remote_copy(
            src_ref=src, dst_ref=dst, send_sem=sems.at[0], recv_sem=sems.at[1],
            device_id=device, device_id_type=pl.DeviceIdType.MESH,
        )
        copy.start()
        return copy

    class Swap:
        def __init__(self, number, src, dst, relay, first):
            self.number, self.src, self.dst, self.relay, self.first = number, src, dst, relay, first

        def near(self, side):
            return right if side == 0 else left

        def chunk(self, ref, k):
            return ref.at[pl.ds(k * CHUNK_ROWS, CHUNK_ROWS)]

        def copy(self, src, dst, send_sem, recv_sem, device):
            return pltpu.make_async_remote_copy(
                src_ref=src, dst_ref=dst, send_sem=send_sem, recv_sem=recv_sem,
                device_id=device, device_id_type=pl.DeviceIdType.MESH,
            )

        def direct(self, side):
            sems = direct_sems.at[self.number, side]
            return self.copy(
                self.src(side).at[self.first], self.dst(side).at[self.first], sems.at[0], sems.at[1], self.near(side)
            )

        def plain(self, side, k):
            sems = chunk_sems.at[self.number, side, k]
            second = self.first + 1
            return self.copy(
                self.chunk(self.src(side).at[second], k), self.chunk(self.dst(side).at[second], k),
                sems.at[0], sems.at[1], self.near(side),
            )

        def detour(self, side, k):
            sems = relay_sems.at[self.number, side, k]
            return self.copy(
                self.chunk(self.src(side).at[self.first + 1], k), self.chunk(self.relay(side), k),
                sems.at[0], sems.at[1], wrapped[side],
            )

        def forwarded(self, side, k):
            return self.copy(
                self.chunk(self.relay(side), k), self.chunk(self.dst(side).at[self.first + 1], k),
                onward_sems.at[self.number, side, k], chunk_sems.at[self.number, side, k].at[1], onward[side],
            )

        def start(self):
            for side in range(2):
                @pl.when(at_end[side])
                def _():
                    for k in range(PIECES):
                        self.detour(side, k).start()

                @pl.when(jnp.logical_not(at_end[side]))
                def _():
                    for k in range(PIECES):
                        self.plain(side, k).start()

            for side in range(2):
                self.direct(side).start()

        def forward(self):
            for side in range(2):
                @pl.when(at_start[side])
                def _():
                    for k in range(PIECES):
                        self.detour(side, k).wait_recv()
                        self.forwarded(side, k).start()

        def wait(self):
            for side in range(2):
                for k in range(PIECES):
                    self.plain(side, k).wait_recv()
                self.direct(side).wait()

                @pl.when(at_end[side])
                def _():
                    for k in range(PIECES):
                        self.detour(side, k).wait_send()

                @pl.when(jnp.logical_not(at_end[side]))
                def _():
                    for k in range(PIECES):
                        self.plain(side, k).wait_send()

                @pl.when(at_start[side])
                def _():
                    for k in range(PIECES):
                        self.forwarded(side, k).wait_send()

    def halo_swap(number, first):
        return Swap(number, lambda side: own_obj, lambda side: halo.at[side], lambda side: halo_relay.at[number, side], first)

    def rim_swap(number, first):
        return Swap(
            number, lambda side: out_codes.at[side], lambda side: in_codes.at[side],
            lambda side: code_relay.at[number - 2, side], first,
        )

    halo_two, halo_one = halo_swap(0, 2), halo_swap(1, 0)
    rim_two, rim_one = rim_swap(2, 2), rim_swap(3, 0)
    halo_two.start()

    at_row = lax.broadcasted_iota(jnp.int32, (PX, PX), 0)
    at_col = lax.broadcasted_iota(jnp.int32, (PX, PX), 1)
    sort_row = (at_col == jnp.where(at_row < HALF, 2 * at_row, 2 * at_row - PX + 1)).astype(f32).astype(bf16)
    sort_col = (at_row == jnp.where(at_col < HALF, 2 * at_col, 2 * at_col - PX + 1)).astype(f32).astype(bf16)
    grad[...] = jnp.zeros_like(grad)
    pad[:, :PX] = jnp.zeros((2, PX, 3 * HALF), f32)
    pad[:, PX + TALL :] = jnp.zeros((2, PX - 8, 3 * HALF), f32)
    obj[:, ROWS:, :] = jnp.zeros((2, 8, 3 * HALF), f32)
    gp[...] = jnp.zeros_like(gp)
    loads[0].wait()

    def sort_amps(p, carry):
        amp = jnp.dot(sort_row, amps[p], preferred_element_type=f32).astype(bf16)
        sorted_amps[p] = jnp.dot(amp, sort_col, preferred_element_type=f32)
        return carry

    lax.fori_loop(0, POSITIONS, sort_amps, 0)
    has_left = jnp.where(t > 0, 1.0, 0.0)
    has_right = jnp.where(t < 63, 1.0, 0.0)

    def widen(first):
        for c in range(2):
            obj[c, :ROWS, :HALF] = halo[0, first + c].astype(f32) * has_left
            obj[c, :ROWS, HALF : 2 * HALF] = own_obj[first + c].astype(f32)
            obj[c, :ROWS, 2 * HALF :] = halo[1, first + c].astype(f32) * has_right

    def offsets(p):
        row_at = row_ref[p]
        return lax.div(row_at, 8), lax.rem(row_at, 8), col_ref[p]

    def take_patch(p, dst):
        row_tile, row_rest, col_at = offsets(p)
        pick = (
            lax.broadcasted_iota(jnp.int32, (3 * HALF, PX), 0)
            == lax.broadcasted_iota(jnp.int32, (3 * HALF, PX), 1) + col_at
        ).astype(f32).astype(bf16)
        for c in range(2):
            raw = obj[c, pl.ds(row_tile * 8, TALL), :].astype(bf16)
            wide = jnp.dot(raw, pick, preferred_element_type=f32)
            dst[c] = pltpu.roll(wide, TALL - row_rest, 0)[:PX]

    def add_patch(p, first, values):
        row_tile, row_rest, col_at = offsets(p)
        place = (
            lax.broadcasted_iota(jnp.int32, (PX, 3 * HALF), 1)
            == lax.broadcasted_iota(jnp.int32, (PX, 3 * HALF), 0) + col_at
        ).astype(f32).astype(bf16)
        for c in range(2):
            high, low = split(values[c])
            moved = jnp.dot(lanes(high, low), rows(place, place), preferred_element_type=f32)
            moved = rows(moved, jnp.zeros((TALL - PX, 3 * HALF), f32))
            pad[c, PX : PX + TALL] = pltpu.roll(moved, row_rest, 0)
            grad[first + c] = grad[first + c] + pad[c, pl.ds((PX // 8 - row_tile) * 8, ROWS), :]

    def send_rims(swap):
        first = swap.first
        copies = []
        for side in range(2):
            from_lane = 2 * HALF * (1 - side)
            for c in range(2):
                quantised(
                    grad[first + c, :, from_lane : from_lane + HALF],
                    out_codes.at[side, first + c], out_scales.at[side, first + c],
                )
        swap.start()
        for side in range(2):
            part = pl.ds(first, 2)
            copies.append(
                send(out_scales.at[side, part], in_scales.at[side, part], scale_sems.at[side, first // 2], swap.near(side))
            )
        return copies

    for load in loads[1:]:
        load.wait()
    halo_two.forward()
    halo_two.wait()
    halo_one.start()
    widen(2)

    def stacked_halves(high, low, product, mixed):
        for r in range(0, HALF, STEP):
            for i in range(2):
                here = pl.ds(r, STEP), slice(i * HALF, i * HALF + HALF)
                there = pl.ds(HALF + r, STEP), slice(i * HALF, i * HALF + HALF)
                u, v = product[0, here[0], here[1]], product[1, here[0], here[1]]
                top = lanes(u + v, u - v) if mixed else lanes(u, v)
                u, v = product[0, there[0], there[1]], product[1, there[0], there[1]]
                bottom = lanes(u + v, u - v) if mixed else lanes(u, v)
                put(high.at[0], low.at[0], i * HALF + r, top + bottom)
                put(high.at[1], low.at[1], i * HALF + r, top - bottom)

    def phase_one(p, carry):
        take_patch(p, patch)
        for m in range(2):
            high, low, product = highs.at[m], lows.at[m], products.at[m]
            for r in range(0, PX, STEP):
                part = pl.ds(r, STEP)
                sr, si = patch[0, part], patch[1, part]
                wr, wi = waves[p, 0, m, part].astype(f32), waves[p, 1, m, part].astype(f32)
                p0, p1 = halves(wr * sr - wi * si, wr * si + wi * sr)
                put(high.at[0], low.at[0], r, p0 + p1)
                put(high.at[1], low.at[1], r, p0 - p1)
            for e in range(2):
                product[e] = by_right(high.at[e], low.at[e], tables, e)
            stacked_halves(high, low, product, False)
            for e in range(2):
                far[m, e] = by_left(high.at[e], low.at[e], tables, 2 + e)
        for e in range(2):
            for r in range(0, HALF, STEP):
                real, imag = pl.ds(r, STEP), pl.ds(HALF + r, STEP)
                zs = [(far[m, e, real], far[m, e, imag]) for m in range(2)]
                power = 0.0
                for zr, zi in zs:
                    power = power + (zr * zr + zi * zi)
                amp = sorted_amps[p, e * HALF + r : e * HALF + r + STEP]
                factor = 1.0 - amp * jnp.minimum(lax.rsqrt(power), 1.0 / floor_level)
                for m, (zr, zi) in enumerate(zs):
                    put(highs.at[m, e], lows.at[m, e], r, zr * factor)
                    put(highs.at[m, e], lows.at[m, e], HALF + r, zi * factor)
        for m in range(2):
            high, low, product = highs.at[m], lows.at[m], products.at[m]
            for e in range(2):
                product[e] = by_left(high.at[e], low.at[e], tables, 4 + e)
            for r in range(0, HALF, STEP):
                real, imag = pl.ds(r, STEP), pl.ds(HALF + r, STEP)
                ur, ui, vr, vi = product[0, real], product[0, imag], product[1, real], product[1, imag]
                for at, re, im in ((r, ur + vr, ui + vi), (HALF + r, ur - vr, ui - vi)):
                    even, odd = halves(re, im)
                    put(high.at[0], low.at[0], at, even)
                    put(high.at[1], low.at[1], at, odd)
            for e in range(2):
                product[e] = by_right(high.at[e], low.at[e], tables, 6 + e)
            for r in range(0, PX, STEP):
                part = pl.ds(r, STEP)
                u, v = product[0, part], product[1, part]
                s, d = u + v, u - v
                cr = lanes(s[:, :HALF], d[:, :HALF])
                ci = lanes(s[:, HALF:], d[:, HALF:])
                sr, si = patch[0, part], patch[1, part]
                wr, wi = waves[p, 0, m, part].astype(f32), waves[p, 1, m, part].astype(f32)
                gr, gi = wr * cr + wi * ci, wr * ci - wi * cr
                if m == 0:
                    upd[p, 0, part], upd[p, 1, part] = gr, gi
                else:
                    upd[p, 0, part], upd[p, 1, part] = upd[p, 0, part] + gr, upd[p, 1, part] + gi
                p0, p1 = halves(sr * cr + si * ci, sr * ci - si * cr)
                put(back_high.at[p, m, 0], back_low.at[p, m, 0], r, p0 + p1)
                put(back_high.at[p, m, 1], back_low.at[p, m, 1], r, p0 - p1)
        add_patch(p, 2, upd.at[p])

        @pl.when(p == 1)
        def _():
            halo_one.forward()

        return carry

    lax.fori_loop(0, POSITIONS, phase_one, 0)
    scale_two = send_rims(rim_two)
    halo_one.wait()
    widen(0)

    def phase_two(p, carry):
        take_patch(p, patch)
        for m in range(2):
            high, low, product = highs.at[m], lows.at[m], products.at[m]
            for e in range(2):
                product[e] = by_right(back_high.at[p, m, e], back_low.at[p, m, e], tables, 8 + e)
            stacked_halves(high, low, product, True)
            for e in range(2):
                far[m, e] = by_left(high.at[e], low.at[e], tables, 10 + e)
        for r in range(0, HALF, STEP):
            real, imag = pl.ds(r, STEP), pl.ds(HALF + r, STEP)
            for bottom in range(2):
                part = pl.ds(bottom * HALF + r, STEP)
                ar, ai = patch[0, part], patch[1, part]
                sum_r, sum_i = 0.0, 0.0
                for m in range(2):
                    ur, ui, vr, vi = far[m, 0, real], far[m, 0, imag], far[m, 1, real], far[m, 1, imag]
                    br, bi = (ur - vr, ui - vi) if bottom else (ur + vr, ui + vi)
                    pr, pi = probe[0, m, part], probe[1, m, part]
                    sum_r = sum_r + (pr * br + pi * bi)
                    sum_i = sum_i + (pr * bi - pi * br)
                    tile_at = (bottom * HALF + r) // 16
                    for c, value in enumerate((ar * br + ai * bi, ar * bi - ai * br)):
                        for h in range(2):
                            half = value[:, h * HALF : (h + 1) * HALF].reshape(STEP // 16, 2, 8, HALF)
                            for l in range(2):
                                to = c * 2 + m, l * 2 + h, pl.ds(tile_at, STEP // 16)
                                gp[to] = gp[to] + half[:, l]
                upd[p, 0, part], upd[p, 1, part] = sum_r, sum_i
        return carry

    def scatter_one(p, carry):
        add_patch(p, 0, upd.at[p])
        return carry

    def finish(copies):
        for copy in copies:
            copy.wait()

    def code_piece(q, carry):
        values = gp[q // 4, q % 4].reshape(HALF, HALF)
        largest = jnp.maximum(jnp.max(jnp.abs(values), axis=0, keepdims=True), 1e-30)
        power = jnp.ceil(jnp.log2(largest))
        scaled = values * (LEVELS_TWO * jnp.exp2(-power))
        probe_codes[q, :HALF] = jnp.round(scaled).astype(jnp.int32).astype(jnp.int16)
        probe_codes[q, HALF:] = jnp.broadcast_to(power, (16, HALF)).astype(jnp.int32).astype(jnp.int16)
        return carry

    lax.fori_loop(0, 1, phase_two, 0)
    rim_two.forward()
    lax.fori_loop(1, POSITIONS, phase_two, 0)
    lax.fori_loop(0, 16, code_piece, 0)
    one = [
        send(probe_codes.at[(spot + j) % 16], r1.at[j - 1], sems3.at[j - 1], along_spot(j)) for j in range(1, 16)
    ]
    lax.fori_loop(0, POSITIONS, scatter_one, 0)
    scale_one = send_rims(rim_one)
    rim_one.forward()
    rim_two.wait()
    finish(scale_two)
    acc = jnp.zeros((8, HALF), f32)

    def total_of(c, acc):
        for k in range(CHUNKS):
            part = pl.ds(k * 64, 64)
            total = grad[c, part, HALF : 2 * HALF]
            total = total + restored(in_codes.at[1, c], in_scales.at[1, c], k) * has_right
            total = total + restored(in_codes.at[0, c], in_scales.at[0, c], k) * has_left
            total_out[c, part] = total
            acc = acc + jnp.sum((total * total).reshape(8, 8, HALF), axis=0)
        return acc

    for c in (2, 3):
        acc = total_of(c, acc)
    finish(one)
    mine = gp[x, g]
    for j in range(15):
        power = r1[j, HALF:].astype(jnp.int32).astype(f32)[:1]
        codes = r1[j, :HALF].astype(jnp.int32).astype(f32)
        mine = mine + (codes * (jnp.exp2(power) * (1.0 / LEVELS_TWO))).reshape(16, 8, HALF)
    s3[...] = mine
    four = [send(s3.at[(zy + j) % 16], r4.at[j - 1], sems4.at[j - 1], along_zy(j)) for j in range(1, 16)]
    rim_one.wait()
    finish(scale_one)
    for c in (0, 1):
        acc = total_of(c, acc)
    finish(four)
    piece = s3[zy]
    for j in range(15):
        piece = piece + r4[j]
    fin[0] = piece
    gathers = [send(fin.at[0], fin.at[j], sems5.at[j - 1], along_group(j)) for j in range(1, 4)]
    object_row = jnp.sum(acc, axis=0, keepdims=True)
    probe_row = jnp.sum(piece * piece, axis=0, keepdims=True)
    top = lax.broadcasted_iota(jnp.int32, (8, HALF), 0) < 4
    q1[0] = jnp.where(top, object_row, probe_row)
    finish([send(q1.at[0], q1.at[j], sems6.at[j - 1], along_zy(j)) for j in range(1, 16)])
    both = q1[zy]
    for s in range(1, 16):
        both = both + q1[(zy + 16 - s) % 16]
    q2[0] = both
    finish([send(q2.at[0], q2.at[j], sems7.at[j - 1], along_spot(j)) for j in range(1, 16)])
    both = q2[spot]
    for s in range(1, 16):
        both = both + q2[(spot + 16 - s) % 16]
    squares_out[...] = both
    finish(gathers)
    for s in range(4):
        shard_out[s // 2 * 8 : s // 2 * 8 + 8, s % 2 * HALF : s % 2 * HALF + HALF] = fin[(g + 4 - s) % 4]


def final_kernel(own_hbm, total_hbm, squares_hbm, shard_hbm, probe_hbm, object_new, probe_new,
                 own_obj, total, squares, shard, old_probe, sems):
    at = pl.multiple_of(lax.axis_index("tile") * 16, 16)
    loads = [
        pltpu.make_async_copy(src, dst, sems.at[i])
        for i, (src, dst) in enumerate([
            (squares_hbm, squares), (total_hbm, total), (own_hbm, own_obj), (shard_hbm, shard),
            (probe_hbm.at[pl.ds(at, 16)], old_probe),
        ])
    ]
    for load in loads:
        load.start()
    for load in loads:
        load.wait()
    sums = jnp.sum(squares[...], axis=1, keepdims=True)
    object_step_size = object_step * lax.rsqrt(sums[0:1] * (1.0 / OBJECT_COUNT) + epsilon)
    probe_step_size = probe_step * lax.rsqrt(sums[4:5] * (1.0 / PROBE_COUNT) + epsilon)
    for c in range(4):
        object_new[c] = own_obj[c].astype(f32) - total[c] * object_step_size
    probe_new[...] = old_probe[...] - shard[...] * probe_step_size


def shards(object_slices, probe, mid_waves, amplitudes, row_offsets, col_offsets):
    tables = jnp.asarray(transform_tables())
    tile = (8, HALF)
    whole = (PX, PX)
    vmem = pl.BlockSpec(memory_space=pltpu.VMEM)
    smem = pl.BlockSpec(memory_space=pltpu.SMEM)
    anywhere = pl.BlockSpec(memory_space=pl.ANY)
    sem = pltpu.SemaphoreType.DMA
    strip = jax.ShapeDtypeStruct(object_slices.shape, f32)
    shard = jax.ShapeDtypeStruct((16, PX), f32)
    total, squares, shard_sum = pl.pallas_call(
        kernel,
        out_shape=[strip, jax.ShapeDtypeStruct(tile, f32), shard],
        in_specs=[smem, smem, vmem] + [anywhere] * 4,
        out_specs=[vmem] * 3,
        scratch_shapes=[
            pltpu.VMEM((2, 2, *whole), f32),
            pltpu.VMEM((3, 2, 2, *whole), bf16),
            pltpu.VMEM((3, *whole), bf16),
            pltpu.VMEM(tables.shape, bf16),
            pltpu.VMEM((2, 4, ROWS, HALF), bf16),
            pltpu.VMEM((2, ROWS + 8, 3 * HALF), f32),
            pltpu.VMEM((4, ROWS, 3 * HALF), f32),
            pltpu.VMEM((2, ROWS + PX, 3 * HALF), f32),
            pltpu.VMEM((2, *whole), f32),
            pltpu.VMEM((2, 2, *whole), f32),
            pltpu.VMEM((3, 2, 2, *whole), bf16),
            pltpu.VMEM((3, 2, 2, *whole), bf16),
            pltpu.VMEM((2, 2, *whole), bf16),
            pltpu.VMEM((2, 2, *whole), bf16),
            pltpu.VMEM((2, 2, *whole), f32),
            pltpu.VMEM((3, 2, *whole), f32),
            pltpu.VMEM((3, *whole), f32),
            pltpu.VMEM((4, 4, 16, *tile), f32),
            pltpu.VMEM((2, 4, ROWS, HALF), jnp.int16),
            pltpu.VMEM((2, 4, *tile), f32),
            pltpu.VMEM((2, 4, ROWS, HALF), jnp.int16),
            pltpu.VMEM((2, 4, *tile), f32),
            pltpu.VMEM((2, 2, ROWS, HALF), bf16),
            pltpu.VMEM((2, 2, ROWS, HALF), jnp.int16),
            pltpu.VMEM((16, HALF + 16, HALF), jnp.int16),
            pltpu.VMEM((15, HALF + 16, HALF), jnp.int16),
            pltpu.VMEM((16, *tile), f32),
            pltpu.VMEM((15, *tile), f32),
            pltpu.VMEM((4, *tile), f32),
            pltpu.VMEM((16, *tile), f32),
            pltpu.VMEM((16, *tile), f32),
            sem((4,)), sem((4, 2, 2)), sem((4, 2, PIECES, 2)), sem((4, 2, PIECES, 2)), sem((4, 2, PIECES)),
            sem((2, 2, 2)),
            sem((15, 2)), sem((15, 2)), sem((3, 2)), sem((15, 2)), sem((15, 2)),
        ],
        compiler_params=pltpu.CompilerParams(
            collective_id=0, has_side_effects=True, vmem_limit_bytes=56 * 1024 * 1024
        ),
        name="update",
    )(
        row_offsets[0, 0], col_offsets[0, 0], object_slices, probe.reshape(2, 2, *whole),
        mid_waves[0, 0], amplitudes[0, 0], tables,
    )
    return pl.pallas_call(
        final_kernel,
        out_shape=[strip, shard],
        in_specs=[anywhere] * 5,
        out_specs=[vmem] * 2,
        scratch_shapes=[
            pltpu.VMEM(object_slices.shape, bf16), pltpu.VMEM(object_slices.shape, f32), pltpu.VMEM(tile, f32),
            pltpu.VMEM((16, PX), f32), pltpu.VMEM((16, PX), f32), sem((5,)),
        ],
        compiler_params=pltpu.CompilerParams(vmem_limit_bytes=16 * 1024 * 1024),
        name="final",
    )(object_slices, total, squares, shard_sum, probe)


def solution(mesh):
    return jax.shard_map(
        shards,
        mesh=mesh,
        in_specs=(
            P(None, "group", "tile"),
            P(),
            P("group", "tile", None, None, None, None, None),
            P("group", "tile", None, None, None),
            P("group", "tile", None),
            P("group", "tile", None),
        ),
        out_specs=(P(None, "group", "tile"), P("tile", None)),
        check_vma=False,
    )
```
